128 devices in a mesh: section: 2 (over core), dp: 16 (over y, x), tensor: 4 (over z).
Axes of the slice: x: 4, y: 4, z: 4, core: 2. Of those that a mesh axis runs over, the one named last changes fastest.
Arguments:
- tokens: bfloat16 [2, 4096, 1024], P(None, ('dp', 'tensor')), may hold values from -6 to 6
- cotangent: bfloat16 [2, 4096, 1024], P(None, ('dp', 'tensor')), may hold values from -6 to 6
- seq_lengths: int32 [16, 2, 4], P('dp'), may hold values from 0 to 256, as said below
- mix_gain: bfloat16 [2, 1024], P('section'), may hold values from 0.5 to 1.5
- query_weight: bfloat16 [2, 1024, 512], P('section', None, 'tensor'), may hold values from -0.1875 to 0.1875
- key_weight: bfloat16 [2, 1024, 128], P('section'), may hold values from -0.1875 to 0.1875
- value_weight: bfloat16 [2, 1024, 128], P('section'), may hold values from -0.1875 to 0.1875
- attn_out_weight: bfloat16 [2, 512, 1024], P('section', 'tensor'), may hold values from -2 to 2
- ssm_gate_weight: bfloat16 [2, 1024, 1536], P('section', None, 'tensor'), may hold values from -0.1875 to 0.1875
- ssm_in_weight: bfloat16 [2, 1024, 1536], P('section', None, 'tensor'), may hold values from -0.1875 to 0.1875
- ssm_state_weight: bfloat16 [2, 1024, 256], P('section'), may hold values from -0.1875 to 0.1875
- ssm_step_weight: bfloat16 [2, 1024, 24], P('section', None, 'tensor'), may hold values from -0.1875 to 0.1875
- conv_inner: bfloat16 [2, 4, 1536], P('section', None, 'tensor'), may hold values from -3 to 3
- conv_state: bfloat16 [2, 4, 256], P('section'), may hold values from -3 to 3
- step_bias: bfloat16 [2, 24], P('section', 'tensor'), may hold values from -5 to -2
- decay_log: bfloat16 [2, 24], P('section', 'tensor'), may hold values from 0 to 2.765625
- skip_gain: bfloat16 [2, 24], P('section', 'tensor'), may hold values from 0.5 to 1.5
- ssm_out_weight: bfloat16 [2, 1536, 1024], P('section', 'tensor'), may hold values from -0.15625 to 0.15625
- ffn_gain: bfloat16 [2, 1024], P('section'), may hold values from 0.5 to 1.5
- ffn_gate_weight: bfloat16 [2, 1024, 2048], P('section', None, 'tensor'), may hold values from -0.1875 to 0.1875
- ffn_up_weight: bfloat16 [2, 1024, 2048], P('section', None, 'tensor'), may hold values from -0.1875 to 0.1875
- ffn_down_weight: bfloat16 [2, 2048, 1024], P('section', 'tensor'), may hold values from -0.125 to 0.125
Outputs:
- layer_out: float32 [2, 2, 4096, 1024], P('section', None, ('dp', 'tensor'))
- input_grad: float32 [2, 2, 4096, 1024], P('section', None, ('dp', 'tensor'))
- grad_mix_gain: float32 [2, 1024], P('section')
- grad_query_weight: float32 [2, 1024, 512], P('section', None, 'tensor')
- grad_key_weight: float32 [2, 1024, 128], P('section')
- grad_value_weight: float32 [2, 1024, 128], P('section')
- grad_attn_out_weight: float32 [2, 512, 1024], P('section', 'tensor')
- grad_ssm_gate_weight: float32 [2, 1024, 1536], P('section', None, 'tensor')
- grad_ssm_in_weight: float32 [2, 1024, 1536], P('section', None, 'tensor')
- grad_ssm_state_weight: float32 [2, 1024, 256], P('section')
- grad_ssm_step_weight: float32 [2, 1024, 24], P('section', None, 'tensor')
- grad_conv_inner: float32 [2, 4, 1536], P('section', None, 'tensor')
- grad_conv_state: float32 [2, 4, 256], P('section')
- grad_step_bias: float32 [2, 24], P('section', 'tensor')
- grad_decay_log: float32 [2, 24], P('section', 'tensor')
- grad_skip_gain: float32 [2, 24], P('section', 'tensor')
- grad_ssm_out_weight: float32 [2, 1536, 1024], P('section', 'tensor')
- grad_ffn_gain: float32 [2, 1024], P('section')
- grad_ffn_gate_weight: float32 [2, 1024, 2048], P('section', None, 'tensor')
- grad_ffn_up_weight: float32 [2, 1024, 2048], P('section', None, 'tensor')
- grad_ffn_down_weight: float32 [2, 2048, 1024], P('section', 'tensor')
The draws below stay inside these ranges and needn't reach their ends.
Inputs may be any that keep to these rules, and one draw needn't show every extreme that they name: `seq_lengths`: for every data group and micro-batch the 4 lengths sum to between 128 and 256; a zero length is an empty slot. In every data group one micro-batch holds a single sequence of 256 tokens.
All inputs are finite; a program needn't handle non-finite values.
Results may differ from the reference program's by a relative error of at most 0.033.
Values may be sent and summed in bfloat16 or wider, within the bound.
No kernel may reach another device: no remote copies, remote signals or barrier semaphores. Data moves between devices by JAX's collectives and lax.ppermute only.
A program may use at most 192 MiB of HBM per device.

```python
import jax
import jax.numpy as jnp
from jax import lax

D = 1024
HQ = 8
KVH = 2
HD = 64
SSM_HEADS = 24
SSM_DIM = 64
STATE = 128
CONV = 4
FF = 2048
MB_TOK = 256
MICRO = 2
SEQS = 4
TOKENS = 4096
N_SECTION = 2
N_DP = 16


def draw_seq_lengths(key, part):
    key = jax.random.fold_in(key, 7)
    key_fill, key_cuts, key_full = jax.random.split(key, 3)
    filled = jax.random.randint(key_fill, (N_DP, MICRO, 1), MB_TOK // 2, MB_TOK + 1)
    fraction = jax.random.randint(key_cuts, (N_DP, MICRO, SEQS - 1), 0, 1024)
    cut_points = jnp.sort(fraction * filled // 1024, axis=-1)
    boundaries = jnp.concatenate([jnp.zeros((N_DP, MICRO, 1), jnp.int32), cut_points, filled], axis=-1)
    lengths = boundaries[:, :, 1:] - boundaries[:, :, :-1]
    chosen = jax.random.randint(key_full, (N_DP, 1, 1), 0, MICRO)
    single = jnp.where(jnp.arange(SEQS, dtype=jnp.int32) == 0, MB_TOK, 0)
    micro_ids = jnp.arange(MICRO, dtype=jnp.int32)[None, :, None]
    return jnp.where(micro_ids == chosen, single[None, None, :], lengths).astype(jnp.int32)


def steps_of(rng, shape, cuts, smallest, high):
    level = 1.0
    for position, parts in cuts:
        heights = jax.random.uniform(jax.random.fold_in(jax.random.fold_in(rng, 6), position), (parts,), jnp.float32, smallest / len(cuts), high / len(cuts))
        level = level * jnp.repeat(jnp.exp(heights), shape[position] // parts).reshape((-1,) + (1,) * (len(shape) - 1 - position))
    return level


def centred(stream_key, extent, scale, reach, pieces=(), kind=jnp.bfloat16):
    level = steps_of(stream_key, extent, pieces, -0.22, 0.18) if pieces else 1.0
    drawn = jax.random.normal(stream_key, extent, jnp.float32) * scale * level
    return jnp.minimum(jnp.maximum(drawn, -reach), reach).astype(kind)


def setup_inputs(seed: int = 0) -> dict:
    splits = jax.random.split(jax.random.key(seed), 23)
    tokens = centred(splits[0], (MICRO, TOKENS, D), 1.0, 6.0, ((1, 64),))
    cotangent = centred(splits[1], (MICRO, TOKENS, D), 1.0, 6.0, ((1, 64),))
    seq_lengths = draw_seq_lengths(jax.random.fold_in(splits[22], 71), 0)
    mix_gain = jnp.clip(1.0 + 0.1 * jax.random.normal(splits[3], (N_SECTION, D), jnp.float32), 0.5, 1.5).astype(jnp.bfloat16)
    query_weight = centred(splits[4], (N_SECTION, D, HQ * HD), D ** -0.5, 0.1875, ((0, 2), (2, 4)))
    key_weight = centred(splits[5], (N_SECTION, D, KVH * HD), D ** -0.5, 0.1875, ((0, 2),))
    value_weight = centred(splits[6], (N_SECTION, D, KVH * HD), D ** -0.5, 0.1875, ((0, 2),))
    attn_out_weight = centred(splits[7], (N_SECTION, HQ * HD, D), (HQ * HD // 64) ** -0.5, 2.0, ((0, 2), (1, 4)))
    ssm_gate_weight = centred(splits[8], (N_SECTION, D, SSM_HEADS * SSM_DIM), D ** -0.5, 0.1875, ((0, 2), (2, 4)))
    ssm_in_weight = centred(splits[9], (N_SECTION, D, SSM_HEADS * SSM_DIM), D ** -0.5, 0.1875, ((0, 2), (2, 4)))
    ssm_state_weight = centred(splits[10], (N_SECTION, D, 2 * STATE), D ** -0.5, 0.1875, ((0, 2),))
    ssm_step_weight = centred(splits[11], (N_SECTION, D, SSM_HEADS), D ** -0.5, 0.1875, ((0, 2), (2, 4)))
    conv_inner = centred(splits[12], (N_SECTION, CONV, SSM_HEADS * SSM_DIM), CONV ** -0.5, 3.0, ((0, 2), (2, 4)))
    conv_state = centred(splits[13], (N_SECTION, CONV, 2 * STATE), CONV ** -0.5, 3.0, ((0, 2),))
    step_bias = jnp.clip(-5.0 + 3.0 * jax.random.uniform(splits[14], (N_SECTION, SSM_HEADS), jnp.float32) ** steps_of(splits[14], (N_SECTION, SSM_HEADS), ((0, 2), (1, 4)), -0.2, 0.2), -5.0, -2.0).astype(jnp.bfloat16)
    decay_log = jnp.clip(2.765625 * jax.random.uniform(splits[15], (N_SECTION, SSM_HEADS), jnp.float32) ** steps_of(splits[15], (N_SECTION, SSM_HEADS), ((0, 2), (1, 4)), -0.2, 0.2), 0.0, 2.765625).astype(jnp.bfloat16)
    skip_gain = jnp.clip(0.5 + 1.0 * jax.random.uniform(splits[16], (N_SECTION, SSM_HEADS), jnp.float32) ** steps_of(splits[16], (N_SECTION, SSM_HEADS), ((0, 2), (1, 4)), -0.2, 0.2), 0.5, 1.5).astype(jnp.bfloat16)
    ssm_out_weight = centred(splits[17], (N_SECTION, SSM_HEADS * SSM_DIM, D), (SSM_HEADS * SSM_DIM) ** -0.5, 0.15625, ((0, 2), (1, 4)))
    ffn_gain = jnp.clip(1.0 + 0.1 * jax.random.normal(splits[18], (N_SECTION, D), jnp.float32), 0.5, 1.5).astype(jnp.bfloat16)
    ffn_gate_weight = centred(splits[19], (N_SECTION, D, FF), D ** -0.5, 0.1875, ((0, 2), (2, 4)))
    ffn_up_weight = centred(splits[20], (N_SECTION, D, FF), D ** -0.5, 0.1875, ((0, 2), (2, 4)))
    ffn_down_weight = centred(splits[21], (N_SECTION, FF, D), FF ** -0.5, 0.125, ((0, 2), (1, 4)))
    return {"tokens": tokens, "cotangent": cotangent, "seq_lengths": seq_lengths, "mix_gain": mix_gain, "query_weight": query_weight, "key_weight": key_weight, "value_weight": value_weight, "attn_out_weight": attn_out_weight, "ssm_gate_weight": ssm_gate_weight, "ssm_in_weight": ssm_in_weight, "ssm_state_weight": ssm_state_weight, "ssm_step_weight": ssm_step_weight, "conv_inner": conv_inner, "conv_state": conv_state, "step_bias": step_bias, "decay_log": decay_log, "skip_gain": skip_gain, "ssm_out_weight": ssm_out_weight, "ffn_gain": ffn_gain, "ffn_gate_weight": ffn_gate_weight, "ffn_up_weight": ffn_up_weight, "ffn_down_weight": ffn_down_weight}


@jax.custom_vjp
def low(v):
    return lax.optimization_barrier(v.astype(jnp.bfloat16)).astype(jnp.float32)

@jax.custom_vjp
def low_back(v):
    return v

def low_keep(v):
    return (low(v), None)

def low_pass(kept, grad):
    return (grad,)

def back_keep(v):
    return (v, None)

def back_low(kept, grad):
    return (low(grad),)
low.defvjp(low_keep, low_pass)
low_back.defvjp(back_keep, back_low)
EPS = 1e-05
HIGHEST = lax.Precision.HIGHEST

def matmul(left, right):
    return jnp.dot(left, right, precision=HIGHEST, preferred_element_type=jnp.float32)

def rms_norm(values, gain):
    return values * lax.rsqrt(lax.optimization_barrier(jnp.mean(values * values, axis=-1, keepdims=True)) + EPS) * gain

def segment_ids(lengths, row_count):
    seq_ends = jnp.cumsum(lengths)
    places = jnp.arange(row_count, dtype=jnp.int32)
    return lax.optimization_barrier(jnp.sum((places[:, None] >= seq_ends[None, :]).astype(jnp.int32), axis=1))

def causal_conv(values, kernel, segments):
    row_count = values.shape[0]
    taps = kernel.shape[0]
    result = values * kernel[taps - 1]
    for back_step in range(1, taps):
        moved = jnp.pad(values[:row_count - back_step], ((back_step, 0), (0, 0)))
        moved_seg = jnp.pad(segments[:row_count - back_step], (back_step, 0), constant_values=-1)
        same_seq = (moved_seg == segments).astype(values.dtype)[:, None]
        result = result + kernel[taps - 1 - back_step] * moved * same_seq
    return result

def attention(normed, query_weight, key_weight, value_weight, attn_out_weight, segments):
    row_count = normed.shape[0]
    head_count = query_weight.shape[1] // HD
    kv_count = key_weight.shape[1] // HD
    queries = low(matmul(normed, query_weight)).reshape(row_count, head_count, HD)
    key_heads = low(matmul(normed, key_weight)).reshape(row_count, kv_count, HD)
    value_heads = low(matmul(normed, value_weight)).reshape(row_count, kv_count, HD)
    key_heads = jnp.repeat(key_heads, head_count // kv_count, axis=1)
    value_heads = jnp.repeat(value_heads, head_count // kv_count, axis=1)
    block_size = min(512, row_count)
    places = jnp.arange(row_count, dtype=jnp.int32)

    def one_block(block_index):
        start_row = block_index * block_size
        query_block = lax.dynamic_slice_in_dim(queries, start_row, block_size, 0)
        seg_block = lax.dynamic_slice_in_dim(segments, start_row, block_size, 0)
        place_block = lax.dynamic_slice_in_dim(places, start_row, block_size, 0)
        allowed = (seg_block[:, None] == segments[None, :]) & (place_block[:, None] >= places[None, :])
        scores = jnp.einsum('thd,shd->hts', query_block, key_heads, precision=HIGHEST) * HD ** (-0.5)
        scores = jnp.where(allowed[None], scores, -1e+30)
        probabilities = low(jax.nn.softmax(scores, axis=-1))
        return jnp.einsum('hts,shd->thd', probabilities, value_heads, precision=HIGHEST)
    mixture = lax.map(jax.checkpoint(one_block), jnp.arange(row_count // block_size, dtype=jnp.int32))
    mixture = low(mixture.reshape(row_count, head_count * HD))
    return matmul(mixture, attn_out_weight)

def state_space(normed, gate_weight, inner_weight, state_weight, step_weight, conv_inner, conv_state, step_bias, decay_log, skip_gain, out_weight, segments):
    row_count = normed.shape[0]
    head_count = step_weight.shape[1]
    gate_raw = matmul(normed, gate_weight).reshape(row_count, head_count, SSM_DIM)
    inner_act = jax.nn.silu(causal_conv(matmul(normed, inner_weight), conv_inner, segments)).reshape(row_count, head_count, SSM_DIM)
    state_act = jax.nn.silu(causal_conv(matmul(normed, state_weight), conv_state, segments))
    b_map = low(state_act[:, :STATE])
    c_map = low(state_act[:, STATE:])
    step_size = jax.nn.softplus(matmul(normed, step_weight) + step_bias)
    log_total = jnp.cumsum(-step_size * jnp.exp(decay_log), axis=0)
    inner_step = low(inner_act * step_size[:, :, None])
    block_size = min(512, row_count)
    places = jnp.arange(row_count, dtype=jnp.int32)

    def one_block(block_index):
        start_row = block_index * block_size
        c_block = lax.dynamic_slice_in_dim(c_map, start_row, block_size, 0)
        total_block = lax.dynamic_slice_in_dim(log_total, start_row, block_size, 0)
        seg_block = lax.dynamic_slice_in_dim(segments, start_row, block_size, 0)
        place_block = lax.dynamic_slice_in_dim(places, start_row, block_size, 0)
        allowed = (seg_block[:, None] == segments[None, :]) & (place_block[:, None] >= places[None, :])
        intersection = matmul(c_block, b_map.T)
        log_gap = total_block.T[:, :, None] - log_total.T[:, None, :]
        decay_part = jnp.exp(jnp.where(allowed[None], log_gap, 0.0))
        weights = low(jnp.where(allowed[None], intersection[None] * decay_part, 0.0))
        return jnp.einsum('hts,shp->thp', weights, inner_step, precision=HIGHEST)
    mixture = lax.map(jax.checkpoint(one_block), jnp.arange(row_count // block_size, dtype=jnp.int32))
    mixture = mixture.reshape(row_count, head_count, SSM_DIM)
    mixture = (mixture + skip_gain[None, :, None] * inner_act) * jax.nn.silu(gate_raw)
    return matmul(low(mixture.reshape(row_count, head_count * SSM_DIM)), out_weight)

def hybrid_layer(hidden_in, segments, params):
    mix_gain, query_weight, key_weight, value_weight, attn_out_weight, ssm_gate_weight, ssm_in_weight, ssm_state_weight, ssm_step_weight, conv_inner, conv_state, step_bias, decay_log, skip_gain, ssm_out_weight, ffn_gain, ffn_gate_weight, ffn_up_weight, ffn_down_weight = params
    normed = low(rms_norm(hidden_in, mix_gain))
    mixture = attention(normed, query_weight, key_weight, value_weight, attn_out_weight, segments) + state_space(normed, ssm_gate_weight, ssm_in_weight, ssm_state_weight, ssm_step_weight, conv_inner, conv_state, step_bias, decay_log, skip_gain, ssm_out_weight, segments)
    middle = hidden_in + low_back(mixture)
    normed_ffn = low(rms_norm(middle, ffn_gain))
    hidden = low(jax.nn.silu(matmul(normed_ffn, ffn_gate_weight)) * matmul(normed_ffn, ffn_up_weight))
    return middle + low_back(matmul(hidden, ffn_down_weight))

def to_blocks(source):
    return source.astype(jnp.float32).reshape(MICRO, N_DP, MB_TOK, D).transpose(1, 0, 2, 3).reshape(N_DP * MICRO, MB_TOK, D)

def from_blocks(source):
    return source.reshape(N_DP, MICRO, MB_TOK, D).transpose(1, 0, 2, 3).reshape(MICRO, N_DP * MB_TOK, D)

def reference(tokens, cotangent, seq_lengths, mix_gain, query_weight, key_weight, value_weight, attn_out_weight, ssm_gate_weight, ssm_in_weight, ssm_state_weight, ssm_step_weight, conv_inner, conv_state, step_bias, decay_log, skip_gain, ssm_out_weight, ffn_gain, ffn_gate_weight, ffn_up_weight, ffn_down_weight):
    params = tuple((weight.astype(jnp.float32) for weight in (mix_gain, query_weight, key_weight, value_weight, attn_out_weight, ssm_gate_weight, ssm_in_weight, ssm_state_weight, ssm_step_weight, conv_inner, conv_state, step_bias, decay_log, skip_gain, ssm_out_weight, ffn_gain, ffn_gate_weight, ffn_up_weight, ffn_down_weight)))
    inputs = to_blocks(tokens)
    lengths = seq_lengths.reshape(N_DP * MICRO, SEQS)
    segment_rows = jax.vmap(lambda length_row: segment_ids(length_row, MB_TOK))(lengths)
    keep_rows = (segment_rows < SEQS).astype(jnp.float32)[:, :, None]
    grad_out = to_blocks(cotangent) * keep_rows

    def forward(inputs, probe, params):
        first_params = tuple((weight[0] for weight in params))
        second_params = tuple((weight[1] for weight in params))

        def one_step(carried, item_row):
            block_in, block_probe, segments = item_row
            first_out = hybrid_layer(block_in, segments, first_params)
            second_out = hybrid_layer(low_back(low(first_out)) + block_probe, segments, second_params)
            return (carried, (first_out, second_out))
        return lax.scan(jax.checkpoint(one_step), jnp.zeros((), jnp.float32), (inputs, probe, segment_rows))[1]
    outputs, pullback = jax.vjp(forward, inputs, jnp.zeros_like(inputs), params)
    grads_in, grads_probe, grads = pullback((jnp.zeros_like(outputs[0]), grad_out))
    layer_out = jnp.stack([from_blocks(outputs[0]), from_blocks(outputs[1])])
    input_grad = jnp.stack([from_blocks(grads_in), from_blocks(grads_probe)])
    return (layer_out, input_grad, grads[0], grads[1], grads[2], grads[3], grads[4], grads[5], grads[6], grads[7], grads[8], grads[9], grads[10], grads[11], grads[12], grads[13], grads[14], grads[15], grads[16], grads[17], grads[18])
```

```python
import functools

import jax
import jax.numpy as jnp
from jax import lax
from jax.experimental import pallas as pl
from jax.experimental.pallas import tpu as pltpu
from jax.sharding import PartitionSpec as P

HQ = 8
KVH = 2
HD = 64
SSM_DIM = 64
STATE = 128
SEQS = 4
EPS = 1e-05

F32 = jnp.float32
BF16 = jnp.bfloat16
EXACT = lax.Precision.HIGHEST

Q0, KV0, G0, I0, S0, T0, IN_COLS = 0, 128, 384, 768, 1152, 1408, 1536
IN_SPANS = (
    (0, 128), (128, 128), (256, 128), (384, 384), (768, 384), (1152, 256), (1408, 128),
)
LANES = 128
SH0, SH1 = 128, 256
INNER = 384

VMEM = pl.BlockSpec(memory_space=pltpu.VMEM)
SMEM = pl.BlockSpec(memory_space=pltpu.SMEM)
HBM = pl.BlockSpec(memory_space=pltpu.HBM)
STREAM = object()
MIB = 1024 * 1024


def dot_nn(a, b, precision=None):
    return lax.dot_general(
        a, b, (((1,), (0,)), ((), ())), precision=precision, preferred_element_type=F32
    )


def dot_nt(a, b, precision=None):
    return lax.dot_general(
        a, b, (((1,), (1,)), ((), ())), precision=precision, preferred_element_type=F32
    )


def dot_tn(a, b):
    return lax.dot_general(a, b, (((0,), (0,)), ((), ())), preferred_element_type=F32)


def sigmoid(v):
    return 1.0 / (1.0 + jnp.exp(-v))


def iota(shape, dim):
    return lax.broadcasted_iota(jnp.int32, shape, dim)


def sequence_ends(info):
    first = 4 + info[0] * SEQS
    ends, total = [], 0
    for j in range(SEQS):
        total = total + info[first + j]
        ends.append(total)
    return ends


def segment_of(places, ends):
    result = jnp.zeros(places.shape, jnp.int32)
    for end in ends:
        result = result + (places >= end).astype(jnp.int32)
    return result


def allowed_pairs(rows, ends):
    t, s = iota((rows, rows), 0), iota((rows, rows), 1)
    return (s <= t) & (segment_of(t, ends) == segment_of(s, ends))


def same_rows(rows, ends):
    t = iota((rows, 1), 0)
    here = segment_of(t, ends)
    return [
        ((segment_of(t - j, ends) == here) & (t >= j)).astype(F32) for j in range(1, 4)
    ]


def conv(raw, kernel, same):
    result = raw * kernel[3:4]
    for j in range(1, 4):
        result = result + kernel[3 - j : 4 - j] * pltpu.roll(raw, j, 0) * same[j - 1]
    return result


def conv_back(grad, raw, kernel, same):
    rows = raw.shape[0]
    grad_raw = grad * kernel[3:4]
    taps = [jnp.sum(grad * raw, axis=0, keepdims=True)]
    for j in range(1, 4):
        kept = grad * same[j - 1]
        grad_raw = grad_raw + kernel[3 - j : 4 - j] * pltpu.roll(kept, rows - j, 0)
        taps.insert(0, jnp.sum(kept * pltpu.roll(raw, j, 0), axis=0, keepdims=True))
    return grad_raw, taps


def start_fetch(layer, info, own, other, held, sem):
    @pl.when(info[0] == layer)
    def _():
        pltpu.make_async_copy(own, held, sem).start()

    @pl.when(info[0] != layer)
    def _():
        pltpu.make_async_copy(other, held, sem).start()

    return pltpu.make_async_copy(own, held, sem)


def pick(layer, info, own, other):
    mine = (info[0] == layer).astype(F32)
    return own[...].astype(F32) * mine + other[...].astype(F32) * (1.0 - mine)


def place(peer, rows):
    return pl.ds(pl.multiple_of(peer * rows, rows), rows)


def assemble(info, pieces, held):
    local = pieces[0].shape[0]
    for k, piece in enumerate(pieces):
        held[place((info[1] + k) % 4, local), :] = piece[...]


def scatter(info, total, outs):
    local = outs[0].shape[0]
    for k, out in enumerate(outs):
        out[...] = total[place((info[1] + k) % 4, local), :].astype(out.dtype)


def ssm_front(proj, small, same, rows):
    pre = {}
    gate = proj[:, G0:I0]
    inner_raw = proj[:, I0:S0]
    state_raw = proj[:, S0:T0]
    kern_inner = small[0:4, 0:INNER]
    kern_state = small[0:4, INNER : INNER + 2 * STATE]
    inner_pre = conv(inner_raw, kern_inner, same)
    state_pre = conv(state_raw, kern_state, same)
    inner_sig = sigmoid(inner_pre)
    state_sig = sigmoid(state_pre)
    inner_act = inner_pre * inner_sig
    state_act = state_pre * state_sig
    z = proj[:, T0:IN_COLS] + small[4:5, 0:LANES]
    step = jnp.maximum(z, 0.0) + jnp.log1p(jnp.exp(-jnp.abs(z)))
    decay = jnp.exp(small[5:6, 0:LANES])
    lower = (iota((rows, rows), 1) <= iota((rows, rows), 0)).astype(F32)
    log_total = dot_nn(lower, -step * decay, EXACT)
    spread = (iota((LANES, INNER), 1) // SSM_DIM == iota((LANES, INNER), 0)).astype(F32)
    step_cols = dot_nn(step, spread, EXACT)
    pre.update(
        gate=gate, inner_raw=inner_raw, state_raw=state_raw, kern_inner=kern_inner,
        kern_state=kern_state, inner_pre=inner_pre, state_pre=state_pre,
        inner_sig=inner_sig, state_sig=state_sig, inner_act=inner_act, z=z, step=step,
        decay=decay, log_total=log_total, spread=spread, step_cols=step_cols,
        b_map=state_act[:, :STATE].astype(BF16), c_map=state_act[:, STATE:].astype(BF16),
        inner_step=(inner_act * step_cols).astype(BF16), skip=small[6:7, 0:INNER],
    )
    return pre


def pack_kernel(*refs):
    sources, (w_in, w_out, sems) = refs[:9], refs[9:]
    targets = [w_in.at[:, at : at + span] for at, span in IN_SPANS]
    targets += [w_out.at[0:LANES], w_out.at[LANES:]]
    copies = [
        pltpu.make_async_copy(source, target, sems.at[i])
        for i, (source, target) in enumerate(zip(sources, targets))
    ]
    for copy in copies:
        copy.start()
    for copy in copies:
        copy.wait()


def keys_values(info, proj):
    second = (info[1] * (KV0 // HD) // (HQ // KVH)).astype(F32)
    pair = [proj[:, KV0 + j * HD : KV0 + (j + 1) * HD] for j in range(4)]
    keys = pair[0] * (1.0 - second) + pair[1] * second
    values = pair[2] * (1.0 - second) + pair[3] * second
    return keys.astype(BF16), values.astype(BF16)


def mixer_forward_kernel(layer, info, x0, x1, x2, x3, small_own, small_other, *refs):
    in_own, in_other, out_own, out_other = refs[:4]
    refs = refs[4:]
    o0, o1, o2, o3, x_out, proj_out, y_out, mixed_out, w_in, w_out, total, sems = refs
    rows = x_out.shape[0]
    wait_in = start_fetch(layer, info, in_own, in_other, w_in, sems.at[0])
    wait_out = start_fetch(layer, info, out_own, out_other, w_out, sems.at[1])
    assemble(info, (x0, x1, x2, x3), x_out)
    small = pick(layer, info, small_own, small_other)
    if layer == 0:
        h = x_out[...].astype(F32)
        r = lax.rsqrt(jnp.mean(h * h, axis=1, keepdims=True) + EPS)
        x_out[...] = (h * r * small[7:8]).astype(BF16)
    ends = sequence_ends(info)
    allowed = allowed_pairs(rows, ends)
    same = same_rows(rows, ends)
    wait_in.wait()
    proj_out[...] = dot_nn(x_out[...], w_in[...])
    proj = proj_out[...]
    keys, values = keys_values(info, proj)
    for head in range(KV0 // HD):
        queries = proj[:, head * HD : (head + 1) * HD].astype(BF16)
        scores = jnp.where(allowed, dot_nt(queries, keys) * HD**-0.5, -1e30)
        weights = jnp.exp(scores - jnp.max(scores, axis=1, keepdims=True))
        weights = weights / jnp.sum(weights, axis=1, keepdims=True)
        total[:, head * HD : (head + 1) * HD] = dot_nn(weights.astype(BF16), values)
    pre = ssm_front(proj, small, same, rows)
    crossing = dot_nt(pre["c_map"], pre["b_map"])
    log_total = pre["log_total"]
    log_rows = jnp.transpose(log_total)
    for head in range(INNER // SSM_DIM):
        cols = slice(head * SSM_DIM, (head + 1) * SSM_DIM)
        gap = log_total[:, head : head + 1] - log_rows[head : head + 1, :]
        decayed = jnp.exp(jnp.where(allowed, gap, 0.0))
        weights = jnp.where(allowed, crossing * decayed, 0.0).astype(BF16)
        y_out[:, cols] = dot_nn(weights, pre["inner_step"][:, cols])
    gate = pre["gate"]
    gated = (y_out[...] + pre["skip"] * pre["inner_act"]) * (gate * sigmoid(gate))
    mixed_out[:, 0:LANES] = total[:, 0:LANES].astype(BF16)
    mixed_out[:, LANES:] = gated.astype(BF16)
    wait_out.wait()
    total[...] = dot_nn(mixed_out[...], w_out[...])
    scatter(info, total, (o0, o1, o2, o3))


def mixer_backward_kernel(layer, info, g0, g1, g2, g3, small_own, small_other, *refs):
    in_own, in_other, out_own, out_other = refs[:4]
    refs = refs[4:]
    x, proj_ref, y_ref, o0, o1, o2, o3, sh0, sh1, sh2, sh3, g_out, d_main, smalls = refs[:14]
    state_taps, w_in, w_out, total, d_proj, wide, columns, shared, sems = refs[14:]
    rows = x.shape[0]
    wait_out = start_fetch(layer, info, out_own, out_other, w_out, sems.at[1])
    wait_in = start_fetch(layer, info, in_own, in_other, w_in, sems.at[0])
    assemble(info, (g0, g1, g2, g3), g_out)
    small = pick(layer, info, small_own, small_other)
    ends = sequence_ends(info)
    allowed = allowed_pairs(rows, ends)
    same = same_rows(rows, ends)
    proj = proj_ref[...]
    wait_out.wait()
    d_mixed = dot_nt(g_out[...], w_out[...])

    keys, values = keys_values(info, proj)
    d_keys = jnp.zeros((rows, HD), F32)
    d_values = jnp.zeros((rows, HD), F32)
    for head in range(KV0 // HD):
        cols = slice(head * HD, (head + 1) * HD)
        queries = proj[:, cols].astype(BF16)
        d_attn = d_mixed[:, cols].astype(BF16)
        scores = jnp.where(allowed, dot_nt(queries, keys) * HD**-0.5, -1e30)
        weights = jnp.exp(scores - jnp.max(scores, axis=1, keepdims=True))
        weights = weights / jnp.sum(weights, axis=1, keepdims=True)
        d_weights = dot_nt(d_attn, values)
        row_sum = jnp.sum(d_weights * weights, axis=1, keepdims=True)
        d_scores = (weights * (d_weights - row_sum) * HD**-0.5).astype(BF16)
        d_proj[:, cols] = dot_nn(d_scores, keys).astype(BF16)
        d_keys = d_keys + dot_tn(d_scores, queries)
        d_values = d_values + dot_tn(weights.astype(BF16), d_attn)
    second = (info[1] * (KV0 // HD) // (HQ // KVH)).astype(F32)
    for j in range(4):
        part = (d_keys if j < 2 else d_values) * (second if j % 2 else 1.0 - second)
        shared[j, :, 0:HD] = part
        d_proj[:, KV0 + j * HD : KV0 + (j + 1) * HD] = part.astype(BF16)

    pre = ssm_front(proj, small, same, rows)
    gate, inner_act, skip = pre["gate"], pre["inner_act"], pre["skip"]
    gate_sig = sigmoid(gate)
    d_ssm = d_mixed[:, LANES:]
    d_o = d_ssm * (gate * gate_sig)
    combined = y_ref[...] + skip * inner_act
    d_gate = d_ssm * combined * (gate_sig * (1.0 + gate * (1.0 - gate_sig)))
    d_proj[:, G0:I0] = d_gate.astype(BF16)
    skip_cols = jnp.sum(d_o * inner_act, axis=0, keepdims=True)
    d_o_low = d_o.astype(BF16)
    b_map, c_map = pre["b_map"], pre["c_map"]
    crossing = dot_nt(c_map, b_map)
    log_total = pre["log_total"]
    log_rows = jnp.transpose(log_total)
    d_crossing = jnp.zeros((rows, rows), F32)
    columns[...] = jnp.zeros_like(columns)
    d_log = jnp.zeros((rows, LANES), F32)
    lane = iota((rows, LANES), 1)
    for head in range(INNER // SSM_DIM):
        cols = slice(head * SSM_DIM, (head + 1) * SSM_DIM)
        gap = log_total[:, head : head + 1] - log_rows[head : head + 1, :]
        decayed = jnp.where(allowed, jnp.exp(jnp.where(allowed, gap, 0.0)), 0.0)
        d_weights = dot_nt(d_o_low[:, cols], pre["inner_step"][:, cols]) * decayed
        weights = (crossing * decayed).astype(BF16)
        wide[:, cols] = dot_tn(weights, d_o_low[:, cols])
        d_crossing = d_crossing + d_weights
        flow = d_weights * crossing
        d_log = d_log + jnp.where(lane == head, jnp.sum(flow, axis=1, keepdims=True), 0.0)
        columns[head : head + 1, :] = jnp.sum(flow, axis=0, keepdims=True)
    d_log = d_log - jnp.transpose(columns[...])
    upper = (iota((rows, rows), 1) >= iota((rows, rows), 0)).astype(F32)
    d_rate = dot_nn(upper, d_log, EXACT)
    step, decay = pre["step"], pre["decay"]
    d_inner_step = wide[...]
    step_part = dot_nt(d_inner_step * inner_act, pre["spread"], EXACT)
    d_z = (step_part - d_rate * decay) * sigmoid(pre["z"])
    d_proj[:, T0:IN_COLS] = d_z.astype(BF16)
    d_inner = d_inner_step * pre["step_cols"] + skip * d_o
    inner_sig, inner_pre = pre["inner_sig"], pre["inner_pre"]
    d_inner = d_inner * (inner_sig * (1.0 + inner_pre * (1.0 - inner_sig)))
    d_inner, inner_taps = conv_back(d_inner, pre["inner_raw"], pre["kern_inner"], same)
    d_proj[:, I0:S0] = d_inner.astype(BF16)
    d_cross_low = d_crossing.astype(BF16)
    wide[:, 0:STATE] = dot_tn(d_cross_low, c_map)
    wide[:, STATE : 2 * STATE] = dot_nn(d_cross_low, b_map)
    state_sig, state_pre = pre["state_sig"], pre["state_pre"]
    d_state = wide[:, 0 : 2 * STATE] * (state_sig * (1.0 + state_pre * (1.0 - state_sig)))
    d_state, taps = conv_back(d_state, pre["state_raw"], pre["kern_state"], same)
    d_proj[:, S0:T0] = d_state.astype(BF16)

    wait_in.wait()
    total[...] = dot_nt(d_proj[...], w_in[...])
    scatter(info, total, (o0, o1, o2, o3))

    for j in range(4):
        shared[j, :, HD:] = d_state[:, j * HD : (j + 1) * HD]
    for k, out in enumerate((sh0, sh1, sh2, sh3)):
        out[...] = shared[(info[1] + k) % 4].astype(BF16)
    d_main[:, 0:KV0] = d_proj[:, 0:KV0]
    d_main[:, SH0:SH1] = jnp.zeros((rows, SH1 - SH0), BF16)
    d_main[:, SH1:] = d_proj[:, G0:S0]
    smalls[...] = jnp.zeros_like(smalls)
    smalls[0:8, :] = dot_tn(d_proj[:, T0:IN_COLS], x[...])[0:8]
    for j in range(4):
        smalls[8 + j : 9 + j, 0:INNER] = inner_taps[j]
        state_taps[j : j + 1, :] = jnp.zeros((1, state_taps.shape[1]), F32)
        state_taps[j : j + 1, 0 : 2 * STATE] = taps[j]
    smalls[12:13, 0:LANES] = jnp.sum(d_z, axis=0, keepdims=True)
    smalls[13:14, 0:LANES] = jnp.sum(-d_rate * step * decay, axis=0, keepdims=True)
    smalls[14:15, 0:INNER] = skip_cols


def feed_forward_kernel(
    layer, info, x0, x1, x2, x3, wg_own, wg_other, wu_own, wu_other, wd_own, wd_other,
    o0, o1, o2, o3, x_out, raw_out, w_gu, w_d, total, sems,
):
    units = w_d.shape[0]
    waits = [
        start_fetch(layer, info, wg_own, wg_other, w_gu.at[:, 0:units], sems.at[0]),
        start_fetch(layer, info, wu_own, wu_other, w_gu.at[:, units:], sems.at[1]),
    ]
    wait_d = start_fetch(layer, info, wd_own, wd_other, w_d, sems.at[2])
    assemble(info, (x0, x1, x2, x3), x_out)
    for item in waits:
        item.wait()
    raw_out[...] = dot_nn(x_out[...], w_gu[...])
    gate = raw_out[:, 0:units]
    hidden = (gate * sigmoid(gate) * raw_out[:, units:]).astype(BF16)
    wait_d.wait()
    total[...] = dot_nn(hidden, w_d[...])
    scatter(info, total, (o0, o1, o2, o3))


def feed_backward_kernel(
    layer, info, g0, g1, g2, g3, raw, wg_own, wg_other, wu_own, wu_other, wd_own, wd_other,
    o0, o1, o2, o3, g_out, d_raw, hidden, w_gu, w_d, total, sems,
):
    units = w_d.shape[0]
    wait_d = start_fetch(layer, info, wd_own, wd_other, w_d, sems.at[2])
    waits = [
        start_fetch(layer, info, wg_own, wg_other, w_gu.at[:, 0:units], sems.at[0]),
        start_fetch(layer, info, wu_own, wu_other, w_gu.at[:, units:], sems.at[1]),
    ]
    assemble(info, (g0, g1, g2, g3), g_out)
    gate, up = raw[:, 0:units], raw[:, units:]
    sig = sigmoid(gate)
    act = gate * sig
    hidden[...] = (act * up).astype(BF16)
    wait_d.wait()
    d_hidden = dot_nt(g_out[...], w_d[...])
    d_raw[:, 0:units] = (d_hidden * up * (sig * (1.0 + gate * (1.0 - sig)))).astype(BF16)
    d_raw[:, units:] = (d_hidden * act).astype(BF16)
    for item in waits:
        item.wait()
    total[...] = dot_nt(d_raw[...], w_gu[...])
    scatter(info, total, (o0, o1, o2, o3))


def sum_norm_kernel(
    layer, gain_row, narrow, info, h, p0, p1, p2, p3, small_own, small_other, total, normed, low
):
    small = pick(layer, info, small_own, small_other)
    value = h[...].astype(F32) + p0[...].astype(F32)
    for part in (p1, p2, p3):
        value = value + part[...].astype(F32)
    total[...] = value
    low[...] = value.astype(BF16)
    if narrow:
        value = low[...].astype(F32)
    r = lax.rsqrt(jnp.mean(value * value, axis=1, keepdims=True) + EPS)
    normed[...] = (value * r * small[gain_row : gain_row + 1]).astype(BF16)


def loss_grad_kernel(info, cotangent, grad, low):
    local = grad.shape[0]
    own = info[1] * local + iota((local, 1), 0)
    kept = (segment_of(own, sequence_ends(info)) < SEQS).astype(F32)
    value = cotangent[info[0]].astype(F32) * kept
    grad[...] = value
    low[...] = value.astype(BF16)


def norm_back_kernel(
    layer, gain_row, info, h, g, p0, p1, p2, p3, small_own, small_other, grad, low, d_gain
):
    small = pick(layer, info, small_own, small_other)
    d_normed = p0[...].astype(F32)
    for part in (p1, p2, p3):
        d_normed = d_normed + part[...].astype(F32)
    value = h[...].astype(F32)
    r = lax.rsqrt(jnp.mean(value * value, axis=1, keepdims=True) + EPS)
    n = value * r
    e = d_normed * small[gain_row : gain_row + 1]
    result = g[...].astype(F32) + r * (e - n * jnp.mean(e * n, axis=1, keepdims=True))
    grad[...] = result
    low[...] = result.astype(BF16)
    d_gain[...] = jnp.sum(d_normed * n, axis=0, keepdims=True)


def half_grads(half, joined, x, d, left, right, parts):
    span = x.shape[1] // 2
    side = left.shape[1] // 2
    xs = x[:, pl.ds(pl.multiple_of(half * span, span), span)]
    ls = left[:, pl.ds(pl.multiple_of(half * side, side), side)]
    grad = d[...]
    if joined:
        shared = sum_parts(parts).astype(BF16)
        grad = jnp.concatenate([grad[:, 0:SH0], shared, grad[:, SH1:]], axis=1)
    return dot_tn(xs, grad), dot_tn(ls, right[...])


def sum_parts(parts):
    total = parts[0][...].astype(F32)
    for part in parts[1:]:
        total = total + part[...].astype(F32)
    return total


def split_factors(groups, refs):
    refs, taken = list(refs), []
    for parts in groups:
        taken.append((refs[:4], refs[4 : 4 + parts]))
        refs = refs[4 + parts :]
    return taken, refs


def send_grad_kernel(groups, info, *rest):
    factors, (out,) = split_factors(groups, rest)
    at = 0
    for four, parts in factors:
        for grad in half_grads(1 - info[0], bool(parts), *four, parts):
            out[at : at + grad.shape[0]] = grad.astype(BF16)
            at += grad.shape[0]


def keep_grad_kernel(groups, info, arrived, *rest):
    factors, (out,) = split_factors(groups, rest)
    at = 0
    for four, parts in factors:
        for grad in half_grads(info[0], bool(parts), *four, parts):
            span = slice(at, at + grad.shape[0])
            out[span] = (grad + arrived[span].astype(F32)).astype(BF16)
            at += grad.shape[0]


def other_layer_kernel(info, second, feed, mixer, out, sems):
    size = feed.shape[0]

    @pl.when(info[0] == 0)
    def _():
        copy = pltpu.make_async_copy(second, out, sems.at[0])
        copy.start()
        copy.wait()

    @pl.when(info[0] != 0)
    def _():
        copies = [
            pltpu.make_async_copy(feed, out.at[0:size], sems.at[0]),
            pltpu.make_async_copy(mixer, out.at[size:], sems.at[1]),
        ]
        for copy in copies:
            copy.start()
        for copy in copies:
            copy.wait()


def spread_feed_kernel(info, own0, own1, other, gate, up, down, held, sems):
    span, side, units = gate.shape[0] // 2, down.shape[0] // 2, gate.shape[1]
    size = held.shape[0]
    wait = start_fetch(0, info, own0, own1.at[0:size], held, sems.at[0])

    def emit(half, source):
        rows = place(half, span)
        gate[rows, :] = source[0:span, 0:units].astype(F32)
        up[rows, :] = source[0:span, units:].astype(F32)
        down[place(half, side), :] = source[span:, :].astype(F32)

    emit(1 - info[0], other.at[0:size])
    wait.wait()
    emit(info[0], held)


def spread_mixer_kernel(info, own0, own1, other, *rest):
    pieces, rest = rest[:4], rest[4:]
    query, key, value, gate, inner, state, attn_out, ssm_out = rest[:8]
    held, shared, outs, sems = rest[8:]
    span, side = query.shape[0] // 2, outs.shape[0] // 2
    size = held.shape[0]
    wait = start_fetch(0, info, own0, own1.at[size:], held, sems.at[0])

    def emit(half, source):
        rows = place(half, span)
        query[rows, :] = source[0:span, 0:SH0].astype(F32)
        gate[rows, :] = source[0:span, SH1 : SH1 + INNER].astype(F32)
        inner[rows, :] = source[0:span, SH1 + INNER :].astype(F32)
        outs[place(half, side), :] = source[span:, :].astype(F32)

    emit(1 - info[0], other.at[size:])
    wait.wait()
    emit(info[0], held)
    attn_out[...] = outs[0:LANES]
    ssm_out[...] = outs[LANES:]
    for k, piece in enumerate(pieces):
        shared[(info[1] + k) % 4] = piece[...].astype(F32)
    for j in range(4):
        into = key if j < 2 else value
        into[:, (j % 2) * HD : (j % 2 + 1) * HD] = shared[j, :, 0:HD]
        state[:, j * HD : (j + 1) * HD] = shared[j, :, HD:]


def run(kernel, specs, args, shapes, scratch=(), flops=10**7, limit=16, after=(), far=()):
    shapes = [jax.ShapeDtypeStruct(*shape) for shape in shapes]
    taken, ordered = len(args), len(args) + len(after)
    given, private = ordered + len(shapes), ordered + len(shapes) + len(scratch)
    near = [i for i, spec in enumerate(specs) if spec is STREAM]
    buffers = [pltpu.VMEM(args[i].shape, args[i].dtype) for i in near]
    buffers += [pltpu.VMEM(shapes[i].shape, shapes[i].dtype) for i in far]
    if buffers:
        buffers.append(pltpu.SemaphoreType.DMA((len(near) + len(far),)))

    def moving_kernel(*refs):
        inputs, outputs = list(refs[:taken]), list(refs[ordered:given])
        copies = []
        for at, i in enumerate(near):
            held = refs[private + at]
            copies.append(pltpu.make_async_copy(inputs[i], held, refs[-1].at[at]))
            inputs[i] = held
        for copy in copies:
            copy.start()
        for copy in copies:
            copy.wait()
        copies = []
        for at, i in enumerate(far, len(near)):
            held = refs[private + at]
            copies.append(pltpu.make_async_copy(held, outputs[i], refs[-1].at[at]))
            outputs[i] = held
        kernel(*inputs, *outputs, *refs[given:private])
        for copy in copies:
            copy.start()
        for copy in copies:
            copy.wait()

    moved = sum(a.size * a.dtype.itemsize for a in list(args) + shapes)
    return list(pl.pallas_call(
        moving_kernel,
        out_shape=shapes,
        in_specs=[HBM if spec is STREAM else spec for spec in specs] + [HBM] * len(after),
        out_specs=[HBM if i in far else VMEM for i in range(len(shapes))],
        scratch_shapes=list(scratch) + buffers,
        compiler_params=pltpu.CompilerParams(vmem_limit_bytes=limit * MIB),
        cost_estimate=pl.CostEstimate(flops=flops, bytes_accessed=moved, transcendentals=0),
    )(*args, *after))


def gather_pieces(piece):
    size = lax.axis_size("tensor")
    return [piece] + [
        lax.ppermute(piece, "tensor", [(i, (i - k) % size) for i in range(size)])
        for k in range(1, size)
    ]


def scatter_pieces(pieces):
    size = lax.axis_size("tensor")
    return [pieces[0]] + [
        lax.ppermute(pieces[k], "tensor", [(i, (i + k) % size) for i in range(size)])
        for k in range(1, size)
    ]


def swap(value):
    return lax.ppermute(value, "section", [(0, 1), (1, 0)])


def dp_pairs(slot, k):
    size = lax.axis_size("dp")
    across = min(4, size)
    stride, count = (1, across) if slot == 2 else (across, size // across)
    pairs = []
    for i in range(size):
        at = i // stride % count
        pairs.append((i, i + ((at + k) % count - at) * stride))
    return pairs


def gather_dp(piece, slot):
    return [piece] + [lax.ppermute(piece, "dp", dp_pairs(slot, 4 - k)) for k in range(1, 4)]


def sum_over_dp(value):
    for slot in (2, 3):
        around = gather_dp(value, slot)
        value = around[0] + around[1] + around[2] + around[3]
    return value


def body(
    tokens,
    cotangent,
    seq_lengths,
    mix_gain,
    query_weight,
    key_weight,
    value_weight,
    attn_out_weight,
    ssm_gate_weight,
    ssm_in_weight,
    ssm_state_weight,
    ssm_step_weight,
    conv_inner,
    conv_state,
    step_bias,
    decay_log,
    skip_gain,
    ssm_out_weight,
    ffn_gain,
    ffn_gate_weight,
    ffn_up_weight,
    ffn_down_weight,
):
    section = lax.axis_index("section")
    tensor = lax.axis_index("tensor")
    local, width = tokens.shape[1], tokens.shape[2]
    rows = local * lax.axis_size("tensor")
    units = ffn_gate_weight.shape[2]
    mixed = attn_out_weight.shape[1] + ssm_out_weight.shape[1]

    dp = lax.axis_index("dp")
    across = min(4, lax.axis_size("dp"))
    place_here = jnp.stack([section, tensor, dp % across, dp // across]).astype(jnp.int32)
    info = jnp.concatenate([place_here, seq_lengths.reshape(-1)])

    def row(vector):
        return jnp.pad(vector, ((0, 0), (0, width - vector.shape[1])))

    small = jnp.concatenate(
        [
            jnp.pad(
                jnp.concatenate([conv_inner[0], conv_state[0]], axis=1),
                ((0, 0), (0, width - INNER - 2 * STATE)),
            ),
            row(step_bias),
            row(decay_log),
            row(jnp.repeat(skip_gain, SSM_DIM, axis=1)),
            mix_gain,
            ffn_gain,
            jnp.zeros((7, width), BF16),
        ],
        axis=0,
    )
    smalls_in = (small, swap(small))
    step_weight = jnp.pad(
        ssm_step_weight[0], ((0, 0), (0, LANES - ssm_step_weight.shape[2]))
    )
    packed = run(
        pack_kernel,
        [HBM] * 9,
        [
            query_weight[0],
            key_weight[0],
            value_weight[0],
            ssm_gate_weight[0],
            ssm_in_weight[0],
            ssm_state_weight[0],
            step_weight,
            attn_out_weight[0],
            ssm_out_weight[0],
        ],
        [((width, IN_COLS), BF16), ((mixed, width), BF16)],
        [pltpu.SemaphoreType.DMA((9,))],
        limit=60,
        far=(0, 1),
    )
    mixer_weights = [packed[0], swap(packed[0]), packed[1], swap(packed[1])]
    feed_weights = []
    for weight in (ffn_gate_weight[0], ffn_up_weight[0], ffn_down_weight[0]):
        feed_weights += [weight, swap(weight)]

    chunk32, chunk16 = ((local, width), F32), ((local, width), BF16)
    full16, full32 = ((rows, width), BF16), ((rows, width), F32)
    mixer_flops = 2 * rows * width * (IN_COLS + mixed)
    feed_flops = 2 * rows * width * 3 * units

    def mixer_scratch():
        return [
            pltpu.VMEM((width, IN_COLS), BF16),
            pltpu.VMEM((mixed, width), BF16),
            pltpu.VMEM((rows, width), F32),
        ]

    def feed_scratch():
        return [
            pltpu.VMEM((width, 2 * units), BF16),
            pltpu.VMEM((units, width), BF16),
            pltpu.VMEM((rows, width), F32),
            pltpu.SemaphoreType.DMA((3,)),
        ]

    loss_grad, loss_low = run(
        loss_grad_kernel, [SMEM, VMEM], [info, cotangent], [chunk32, chunk16]
    )
    loss_pieces = gather_pieces(loss_low)

    layer_in = normed = lax.dynamic_index_in_dim(tokens, section, 0, keepdims=False)
    saved, layer_totals, layer_lows = [], [], []
    for layer in range(2):
        result = run(
            functools.partial(mixer_forward_kernel, layer),
            [SMEM] + [VMEM] * 6 + [HBM] * 4,
            [info, *gather_pieces(normed), *smalls_in, *mixer_weights],
            [chunk32] + [chunk16] * 3
            + [full16, ((rows, IN_COLS), F32), ((rows, INNER), F32), ((rows, mixed), BF16)],
            mixer_scratch() + [pltpu.SemaphoreType.DMA((2,))],
            mixer_flops,
            32,
            far=(4, 5, 6, 7),
        )
        x, proj, y, heads = result[4:]
        middle, normed, _ = run(
            functools.partial(sum_norm_kernel, layer, 8, False),
            [SMEM] + [VMEM] * 7,
            [info, layer_in, *scatter_pieces(result[:4]), *smalls_in],
            [chunk32, chunk16, chunk16],
        )
        result = run(
            functools.partial(feed_forward_kernel, layer),
            [SMEM] + [VMEM] * 4 + [HBM] * 6,
            [info, *gather_pieces(normed), *feed_weights],
            [chunk32] + [chunk16] * 3 + [full16, ((rows, 2 * units), F32)],
            feed_scratch(),
            feed_flops,
            32,
            far=(4, 5),
        )
        feed_x, feed_raw = result[4:]
        total, normed, low = run(
            functools.partial(sum_norm_kernel, 1, 7, True),
            [SMEM] + [VMEM] * 7,
            [info, middle, *scatter_pieces(result[:4]), *smalls_in],
            [chunk32, chunk16, chunk16],
        )
        layer_totals.append(total)
        layer_lows.append(low)
        saved.append((layer_in, x, proj, y, heads, middle, feed_x, feed_raw))
        layer_in = low

    group = (width // 2 + units // 2, width)

    def send_grads(groups, after=()):
        operands = [item for group_items in groups for item in group_items]
        return run(
            functools.partial(send_grad_kernel, [len(items) - 4 for items in groups]),
            [SMEM] + grad_specs(groups),
            [info] + operands,
            [((len(groups) * group[0], width), BF16)],
            (),
            len(groups) * rows * width * (width + units),
            24,
            after=after,
        )[0]

    def grad_specs(groups):
        specs = []
        for items in groups:
            specs += [STREAM] * 4 + [VMEM] * (len(items) - 4)
        return specs

    def keep_grads(send, groups, after=()):
        operands = [item for group_items in groups for item in group_items]
        return run(
            functools.partial(keep_grad_kernel, [len(items) - 4 for items in groups]),
            [SMEM, VMEM] + grad_specs(groups),
            [info, swap(send)] + operands,
            [((len(groups) * group[0], width), BF16)],
            (),
            len(groups) * rows * width * (width + units),
            32,
            after=after,
        )

    grad, pieces = loss_grad, loss_pieces
    smalls, shared_smalls, grads_in, lows_in = {}, {}, {}, {}
    feed_after, middle_after, feed_kept = [], [], []
    for layer in (1, 0):
        layer_in, x, proj, y, heads, middle, feed_x, feed_raw = saved[layer]
        result = run(
            functools.partial(feed_backward_kernel, layer),
            [SMEM] + [VMEM] * 4 + [STREAM] + [HBM] * 6,
            [info, *pieces, feed_raw, *feed_weights],
            [chunk32] + [chunk16] * 3 + [full16, full16, ((rows, units), BF16)],
            feed_scratch(),
            feed_flops,
            32,
            after=feed_after,
            far=(4, 5, 6),
        )
        g_full, d_raw, hidden = result[4:]
        parts = scatter_pieces(result[:4])
        feed_factors = [feed_x, d_raw, hidden, g_full]
        if layer == 0:
            feed_send = send_grads([feed_factors])
            middle_after = [feed_send] + middle_after
        d_middle, d_low, ffn_gain_grad = run(
            functools.partial(norm_back_kernel, layer, 8),
            [SMEM] + [VMEM] * 8,
            [info, middle, grad, *parts, *smalls_in],
            [chunk32, chunk16, ((1, width), F32)],
            after=middle_after,
        )
        if layer == 0:
            feed_kept = keep_grads(feed_send, [feed_factors])
        result = run(
            functools.partial(mixer_backward_kernel, layer),
            [SMEM] + [VMEM] * 6 + [HBM] * 4 + [STREAM] * 3,
            [info, *gather_pieces(d_low), *smalls_in, *mixer_weights, x, proj, y],
            [chunk32] + [chunk16] * 3 + [((rows, LANES), BF16)] * 4
            + [full16, full16, ((16, width), F32), ((4, width), F32)],
            mixer_scratch()
            + [
                pltpu.VMEM((rows, IN_COLS), BF16),
                pltpu.VMEM((rows, INNER), F32),
                pltpu.VMEM((LANES, rows), F32),
                pltpu.VMEM((4, rows, LANES), F32),
                pltpu.SemaphoreType.DMA((2,)),
            ],
            2 * mixer_flops,
            40,
            after=feed_kept,
            far=(8, 9),
        )
        parts = scatter_pieces(result[:4])
        g_full, d_main, smalls[layer], taps = result[8:]
        mixer_factors = [x, d_main, heads, g_full] + scatter_pieces(result[4:8])
        if layer == 1:
            groups = [feed_factors, mixer_factors]
            send = send_grads(groups)
            second_kept = keep_grads(send, groups)
            feed_after, middle_after = [send], second_kept
        else:
            mixer_kept = keep_grads(send_grads([mixer_factors]), [mixer_factors])
            second, feed, mixer = lax.psum(
                (second_kept[0], feed_kept[0], mixer_kept[0]), "dp"
            )
        grad_in, grad, mix_gain_grad = run(
            functools.partial(norm_back_kernel, layer, 7),
            [SMEM] + [VMEM] * 8,
            [info, layer_in, d_middle, *parts, *smalls_in],
            [chunk32, chunk16, ((1, width), F32)],
        )
        grads_in[layer], lows_in[layer] = grad_in, grad
        shared_smalls[layer] = jnp.concatenate(
            [ffn_gain_grad, mix_gain_grad, taps, jnp.zeros((2, width), F32)], axis=0
        )
        if layer == 1:
            pieces = gather_pieces(grad)

    first = section == 0

    shared_pair = jnp.concatenate([shared_smalls[0], shared_smalls[1]], axis=0)
    around = gather_pieces(shared_pair)
    shared_pair = around[0] + around[1] + around[2] + around[3]
    by_layer = [
        jnp.concatenate([smalls[layer], shared_pair[8 * layer : 8 * layer + 8]], axis=0)
        for layer in range(2)
    ]
    small_sum = jnp.where(first, by_layer[0], by_layer[1]) + swap(
        jnp.where(first, by_layer[1], by_layer[0])
    )
    small_sum = sum_over_dp(small_sum)

    def to_layer(totals, lows):
        own_rows = jnp.where(first, totals[0], totals[1])
        other_rows = swap(jnp.where(first, lows[1], lows[0])).astype(F32)
        return jnp.stack(
            [jnp.where(first, own_rows, other_rows), jnp.where(first, other_rows, own_rows)]
        )[None]

    outputs = to_layer(layer_totals, layer_lows)
    inputs = to_layer(grads_in, lows_in)

    (sent,) = run(
        other_layer_kernel,
        [SMEM] + [HBM] * 3,
        [info, second, feed, mixer],
        [((2 * group[0], width), BF16)],
        [pltpu.SemaphoreType.DMA((2,))],
        10**6,
        16,
        after=[small_sum, outputs, inputs],
    )
    other = swap(sent)
    picked = slice(0, width // 2), slice(SH0, SH1)
    own_shared = jnp.where(first, mixer[picked], second[group[0] :][picked])
    other_shared = other[group[0] :][picked]
    shared = jnp.concatenate(
        [
            jnp.where(first, own_shared, other_shared),
            jnp.where(first, other_shared, own_shared),
        ],
        axis=0,
    )
    gate_grad, up_grad, down_grad = run(
        spread_feed_kernel,
        [SMEM, HBM, HBM, VMEM],
        [info, feed, second, other],
        [((width, units), F32), ((width, units), F32), ((units, width), F32)],
        [pltpu.VMEM(group, BF16), pltpu.SemaphoreType.DMA((1,))],
        10**6,
        24,
    )
    mixer_grads = run(
        spread_mixer_kernel,
        [SMEM, HBM, HBM, VMEM] + [VMEM] * 4,
        [info, mixer, second, other, *gather_pieces(shared)],
        [
            ((width, KV0), F32),
            ((width, KVH * HD), F32),
            ((width, KVH * HD), F32),
            ((width, INNER), F32),
            ((width, INNER), F32),
            ((width, 2 * STATE), F32),
            ((LANES, width), F32),
            ((INNER, width), F32),
        ],
        [
            pltpu.VMEM(group, BF16),
            pltpu.VMEM((4, width, LANES), F32),
            pltpu.VMEM((mixed, width), F32),
            pltpu.SemaphoreType.DMA((1,)),
        ],
        10**6,
        32,
    )
    query_grad, key_grad, value_grad, gate_in_grad, inner_grad, state_grad, ao_grad, so_grad = (
        mixer_grads
    )

    heads_here = step_bias.shape[1]
    return (
        outputs,
        inputs,
        small_sum[17:18],
        query_grad[None],
        key_grad[None],
        value_grad[None],
        ao_grad[None],
        gate_in_grad[None],
        inner_grad[None],
        state_grad[None],
        small_sum[0:heads_here].T[None],
        small_sum[8:12, 0:INNER][None],
        small_sum[18:22, 0 : 2 * STATE][None],
        small_sum[12:13, 0:heads_here],
        small_sum[13:14, 0:heads_here],
        jnp.sum(small_sum[14:15, 0:INNER].reshape(heads_here, SSM_DIM), axis=1)[None],
        so_grad[None],
        small_sum[16:17],
        gate_grad[None],
        up_grad[None],
        down_grad[None],
    )


def solution(mesh):
    placed = (
        P(None, ("dp", "tensor"), None),
        P(None, ("dp", "tensor"), None),
        P("dp", None, None),
        P("section", None),
        P("section", None, "tensor"),
        P("section", None, None),
        P("section", None, None),
        P("section", "tensor", None),
        P("section", None, "tensor"),
        P("section", None, "tensor"),
        P("section", None, None),
        P("section", None, "tensor"),
        P("section", None, "tensor"),
        P("section", None, None),
        P("section", "tensor"),
        P("section", "tensor"),
        P("section", "tensor"),
        P("section", "tensor", None),
        P("section", None),
        P("section", None, "tensor"),
        P("section", None, "tensor"),
        P("section", "tensor", None),
    )
    return jax.shard_map(
        body,
        mesh=mesh,
        in_specs=placed,
        out_specs=(
            P("section", None, ("dp", "tensor"), None),
            P("section", None, ("dp", "tensor"), None),
            P("section", None),
            P("section", None, "tensor"),
            P("section", None, None),
            P("section", None, None),
            P("section", "tensor", None),
            P("section", None, "tensor"),
            P("section", None, "tensor"),
            P("section", None, None),
            P("section", None, "tensor"),
            P("section", None, "tensor"),
            P("section", None, None),
            P("section", "tensor"),
            P("section", "tensor"),
            P("section", "tensor"),
            P("section", "tensor", None),
            P("section", None),
            P("section", None, "tensor"),
            P("section", None, "tensor"),
            P("section", "tensor", None),
        ),
        check_vma=False,
    )
```

```python
import functools

import jax
import jax.numpy as jnp
from jax import lax
from jax.experimental import pallas as pl
from jax.experimental.pallas import tpu as pltpu
from jax.sharding import PartitionSpec as P

HQ = 8
KVH = 2
HD = 64
SSM_DIM = 64
STATE = 128
SEQS = 4
EPS = 1e-05

F32 = jnp.float32
BF16 = jnp.bfloat16
EXACT = lax.Precision.HIGHEST

Q0, KV0, G0, I0, S0, T0, IN_COLS = 0, 128, 384, 768, 1152, 1408, 1536
IN_SPANS = (
    (0, 128), (128, 128), (256, 128), (384, 384), (768, 384), (1152, 256), (1408, 128),
)
LANES = 128
SH0, SH1 = 128, 256
INNER = 384

VMEM = pl.BlockSpec(memory_space=pltpu.VMEM)
SMEM = pl.BlockSpec(memory_space=pltpu.SMEM)
HBM = pl.BlockSpec(memory_space=pltpu.HBM)
ANY = pl.BlockSpec(memory_space=pl.ANY)
STREAM = object()
MIB = 1024 * 1024


def dot_nn(a, b, precision=None):
    return lax.dot_general(
        a, b, (((1,), (0,)), ((), ())), precision=precision, preferred_element_type=F32
    )


def dot_nt(a, b, precision=None):
    return lax.dot_general(
        a, b, (((1,), (1,)), ((), ())), precision=precision, preferred_element_type=F32
    )


def dot_tn(a, b):
    return lax.dot_general(a, b, (((0,), (0,)), ((), ())), preferred_element_type=F32)


def sigmoid(v):
    return 1.0 / (1.0 + jnp.exp(-v))


def iota(shape, dim):
    return lax.broadcasted_iota(jnp.int32, shape, dim)


def sequence_ends(info):
    first = 4 + info[0] * SEQS
    ends, total = [], 0
    for j in range(SEQS):
        total = total + info[first + j]
        ends.append(total)
    return ends


def segment_of(places, ends):
    result = jnp.zeros(places.shape, jnp.int32)
    for end in ends:
        result = result + (places >= end).astype(jnp.int32)
    return result


def allowed_pairs(rows, ends):
    t, s = iota((rows, rows), 0), iota((rows, rows), 1)
    return (s <= t) & (segment_of(t, ends) == segment_of(s, ends))


def same_rows(rows, ends):
    t = iota((rows, 1), 0)
    here = segment_of(t, ends)
    return [
        ((segment_of(t - j, ends) == here) & (t >= j)).astype(F32) for j in range(1, 4)
    ]


def conv(raw, kernel, same):
    result = raw * kernel[3:4]
    for j in range(1, 4):
        result = result + kernel[3 - j : 4 - j] * pltpu.roll(raw, j, 0) * same[j - 1]
    return result


def conv_back(grad, raw, kernel, same):
    rows = raw.shape[0]
    grad_raw = grad * kernel[3:4]
    taps = [jnp.sum(grad * raw, axis=0, keepdims=True)]
    for j in range(1, 4):
        kept = grad * same[j - 1]
        grad_raw = grad_raw + kernel[3 - j : 4 - j] * pltpu.roll(kept, rows - j, 0)
        taps.insert(0, jnp.sum(kept * pltpu.roll(raw, j, 0), axis=0, keepdims=True))
    return grad_raw, taps


def start_fetch(layer, info, own, other, held, sem):
    @pl.when(info[0] == layer)
    def _():
        pltpu.make_async_copy(own, held, sem).start()

    @pl.when(info[0] != layer)
    def _():
        pltpu.make_async_copy(other, held, sem).start()

    return pltpu.make_async_copy(own, held, sem)


def pick(layer, info, own, other):
    mine = (info[0] == layer).astype(F32)
    return own[...].astype(F32) * mine + other[...].astype(F32) * (1.0 - mine)


def place(peer, rows):
    return pl.ds(pl.multiple_of(peer * rows, rows), rows)


def assemble(info, pieces, held):
    local = pieces[0].shape[0]
    for k, piece in enumerate(pieces):
        held[place((info[1] + k) % 4, local), :] = piece[...]


def scatter(info, total, outs):
    local = outs[0].shape[0]
    for k, out in enumerate(outs):
        out[...] = total[place((info[1] + k) % 4, local), :].astype(out.dtype)


def ssm_front(proj, small, same, rows):
    pre = {}
    gate = proj[:, G0:I0]
    inner_raw = proj[:, I0:S0]
    state_raw = proj[:, S0:T0]
    kern_inner = small[0:4, 0:INNER]
    kern_state = small[0:4, INNER : INNER + 2 * STATE]
    inner_pre = conv(inner_raw, kern_inner, same)
    state_pre = conv(state_raw, kern_state, same)
    inner_sig = sigmoid(inner_pre)
    state_sig = sigmoid(state_pre)
    inner_act = inner_pre * inner_sig
    state_act = state_pre * state_sig
    z = proj[:, T0:IN_COLS] + small[4:5, 0:LANES]
    step = jnp.maximum(z, 0.0) + jnp.log1p(jnp.exp(-jnp.abs(z)))
    decay = jnp.exp(small[5:6, 0:LANES])
    lower = (iota((rows, rows), 1) <= iota((rows, rows), 0)).astype(F32)
    log_total = dot_nn(lower, -step * decay, EXACT)
    spread = (iota((LANES, INNER), 1) // SSM_DIM == iota((LANES, INNER), 0)).astype(F32)
    step_cols = dot_nn(step, spread, EXACT)
    pre.update(
        gate=gate, inner_raw=inner_raw, state_raw=state_raw, kern_inner=kern_inner,
        kern_state=kern_state, inner_pre=inner_pre, state_pre=state_pre,
        inner_sig=inner_sig, state_sig=state_sig, inner_act=inner_act, z=z, step=step,
        decay=decay, log_total=log_total, spread=spread, step_cols=step_cols,
        b_map=state_act[:, :STATE].astype(BF16), c_map=state_act[:, STATE:].astype(BF16),
        inner_step=(inner_act * step_cols).astype(BF16), skip=small[6:7, 0:INNER],
    )
    return pre


def pack_kernel(*refs):
    sources, (w_in, w_out, sems) = refs[:9], refs[9:]
    targets = [w_in.at[:, at : at + span] for at, span in IN_SPANS]
    targets += [w_out.at[0:LANES], w_out.at[LANES:]]
    copies = [
        pltpu.make_async_copy(source, target, sems.at[i])
        for i, (source, target) in enumerate(zip(sources, targets))
    ]
    for copy in copies:
        copy.start()
    for copy in copies:
        copy.wait()


def keys_values(info, proj):
    second = (info[1] * (KV0 // HD) // (HQ // KVH)).astype(F32)
    pair = [proj[:, KV0 + j * HD : KV0 + (j + 1) * HD] for j in range(4)]
    keys = pair[0] * (1.0 - second) + pair[1] * second
    values = pair[2] * (1.0 - second) + pair[3] * second
    return keys.astype(BF16), values.astype(BF16)


def mixer_forward_kernel(layer, info, x0, x1, x2, x3, small_own, small_other, *refs):
    in_own, in_other, out_own, out_other = refs[:4]
    refs = refs[4:]
    o0, o1, o2, o3, x_out, proj_out, y_out, mixed_out, w_in, w_out, total, sems = refs
    rows = x_out.shape[0]
    wait_in = start_fetch(layer, info, in_own, in_other, w_in, sems.at[0])
    wait_out = start_fetch(layer, info, out_own, out_other, w_out, sems.at[1])
    assemble(info, (x0, x1, x2, x3), x_out)
    small = pick(layer, info, small_own, small_other)
    if layer == 0:
        h = x_out[...].astype(F32)
        r = lax.rsqrt(jnp.mean(h * h, axis=1, keepdims=True) + EPS)
        x_out[...] = (h * r * small[7:8]).astype(BF16)
    ends = sequence_ends(info)
    allowed = allowed_pairs(rows, ends)
    same = same_rows(rows, ends)
    wait_in.wait()
    proj_out[...] = dot_nn(x_out[...], w_in[...])
    proj = proj_out[...]
    keys, values = keys_values(info, proj)
    for head in range(KV0 // HD):
        queries = proj[:, head * HD : (head + 1) * HD].astype(BF16)
        scores = jnp.where(allowed, dot_nt(queries, keys) * HD**-0.5, -1e30)
        weights = jnp.exp(scores - jnp.max(scores, axis=1, keepdims=True))
        weights = weights / jnp.sum(weights, axis=1, keepdims=True)
        total[:, head * HD : (head + 1) * HD] = dot_nn(weights.astype(BF16), values)
    pre = ssm_front(proj, small, same, rows)
    crossing = dot_nt(pre["c_map"], pre["b_map"])
    log_total = pre["log_total"]
    log_rows = jnp.transpose(log_total)
    for head in range(INNER // SSM_DIM):
        cols = slice(head * SSM_DIM, (head + 1) * SSM_DIM)
        gap = log_total[:, head : head + 1] - log_rows[head : head + 1, :]
        decayed = jnp.exp(jnp.where(allowed, gap, 0.0))
        weights = jnp.where(allowed, crossing * decayed, 0.0).astype(BF16)
        y_out[:, cols] = dot_nn(weights, pre["inner_step"][:, cols])
    gate = pre["gate"]
    gated = (y_out[...] + pre["skip"] * pre["inner_act"]) * (gate * sigmoid(gate))
    mixed_out[:, 0:LANES] = total[:, 0:LANES].astype(BF16)
    mixed_out[:, LANES:] = gated.astype(BF16)
    wait_out.wait()
    total[...] = dot_nn(mixed_out[...], w_out[...])
    scatter(info, total, (o0, o1, o2, o3))


def mixer_backward_kernel(layer, info, g0, g1, g2, g3, small_own, small_other, *refs):
    in_own, in_other, out_own, out_other = refs[:4]
    refs = refs[4:]
    x, proj_ref, y_ref, o0, o1, o2, o3, sh0, sh1, sh2, sh3, g_out, d_main, smalls = refs[:14]
    state_taps, w_in, w_out, total, d_proj, wide, columns, shared, sems = refs[14:]
    rows = x.shape[0]
    wait_out = start_fetch(layer, info, out_own, out_other, w_out, sems.at[1])
    wait_in = start_fetch(layer, info, in_own, in_other, w_in, sems.at[0])
    assemble(info, (g0, g1, g2, g3), g_out)
    small = pick(layer, info, small_own, small_other)
    ends = sequence_ends(info)
    allowed = allowed_pairs(rows, ends)
    same = same_rows(rows, ends)
    proj = proj_ref[...]
    wait_out.wait()
    d_mixed = dot_nt(g_out[...], w_out[...])

    keys, values = keys_values(info, proj)
    d_keys = jnp.zeros((rows, HD), F32)
    d_values = jnp.zeros((rows, HD), F32)
    for head in range(KV0 // HD):
        cols = slice(head * HD, (head + 1) * HD)
        queries = proj[:, cols].astype(BF16)
        d_attn = d_mixed[:, cols].astype(BF16)
        scores = jnp.where(allowed, dot_nt(queries, keys) * HD**-0.5, -1e30)
        weights = jnp.exp(scores - jnp.max(scores, axis=1, keepdims=True))
        weights = weights / jnp.sum(weights, axis=1, keepdims=True)
        d_weights = dot_nt(d_attn, values)
        row_sum = jnp.sum(d_weights * weights, axis=1, keepdims=True)
        d_scores = (weights * (d_weights - row_sum) * HD**-0.5).astype(BF16)
        d_proj[:, cols] = dot_nn(d_scores, keys).astype(BF16)
        d_keys = d_keys + dot_tn(d_scores, queries)
        d_values = d_values + dot_tn(weights.astype(BF16), d_attn)
    second = (info[1] * (KV0 // HD) // (HQ // KVH)).astype(F32)
    for j in range(4):
        part = (d_keys if j < 2 else d_values) * (second if j % 2 else 1.0 - second)
        shared[j, :, 0:HD] = part
        d_proj[:, KV0 + j * HD : KV0 + (j + 1) * HD] = part.astype(BF16)

    pre = ssm_front(proj, small, same, rows)
    gate, inner_act, skip = pre["gate"], pre["inner_act"], pre["skip"]
    gate_sig = sigmoid(gate)
    d_ssm = d_mixed[:, LANES:]
    d_o = d_ssm * (gate * gate_sig)
    combined = y_ref[...] + skip * inner_act
    d_gate = d_ssm * combined * (gate_sig * (1.0 + gate * (1.0 - gate_sig)))
    d_proj[:, G0:I0] = d_gate.astype(BF16)
    skip_cols = jnp.sum(d_o * inner_act, axis=0, keepdims=True)
    d_o_low = d_o.astype(BF16)
    b_map, c_map = pre["b_map"], pre["c_map"]
    crossing = dot_nt(c_map, b_map)
    log_total = pre["log_total"]
    log_rows = jnp.transpose(log_total)
    d_crossing = jnp.zeros((rows, rows), F32)
    columns[...] = jnp.zeros_like(columns)
    d_log = jnp.zeros((rows, LANES), F32)
    lane = iota((rows, LANES), 1)
    for head in range(INNER // SSM_DIM):
        cols = slice(head * SSM_DIM, (head + 1) * SSM_DIM)
        gap = log_total[:, head : head + 1] - log_rows[head : head + 1, :]
        decayed = jnp.where(allowed, jnp.exp(jnp.where(allowed, gap, 0.0)), 0.0)
        d_weights = dot_nt(d_o_low[:, cols], pre["inner_step"][:, cols]) * decayed
        weights = (crossing * decayed).astype(BF16)
        wide[:, cols] = dot_tn(weights, d_o_low[:, cols])
        d_crossing = d_crossing + d_weights
        flow = d_weights * crossing
        d_log = d_log + jnp.where(lane == head, jnp.sum(flow, axis=1, keepdims=True), 0.0)
        columns[head : head + 1, :] = jnp.sum(flow, axis=0, keepdims=True)
    d_log = d_log - jnp.transpose(columns[...])
    upper = (iota((rows, rows), 1) >= iota((rows, rows), 0)).astype(F32)
    d_rate = dot_nn(upper, d_log, EXACT)
    step, decay = pre["step"], pre["decay"]
    d_inner_step = wide[...]
    step_part = dot_nt(d_inner_step * inner_act, pre["spread"], EXACT)
    d_z = (step_part - d_rate * decay) * sigmoid(pre["z"])
    d_proj[:, T0:IN_COLS] = d_z.astype(BF16)
    d_inner = d_inner_step * pre["step_cols"] + skip * d_o
    inner_sig, inner_pre = pre["inner_sig"], pre["inner_pre"]
    d_inner = d_inner * (inner_sig * (1.0 + inner_pre * (1.0 - inner_sig)))
    d_inner, inner_taps = conv_back(d_inner, pre["inner_raw"], pre["kern_inner"], same)
    d_proj[:, I0:S0] = d_inner.astype(BF16)
    d_cross_low = d_crossing.astype(BF16)
    wide[:, 0:STATE] = dot_tn(d_cross_low, c_map)
    wide[:, STATE : 2 * STATE] = dot_nn(d_cross_low, b_map)
    state_sig, state_pre = pre["state_sig"], pre["state_pre"]
    d_state = wide[:, 0 : 2 * STATE] * (state_sig * (1.0 + state_pre * (1.0 - state_sig)))
    d_state, taps = conv_back(d_state, pre["state_raw"], pre["kern_state"], same)
    d_proj[:, S0:T0] = d_state.astype(BF16)

    wait_in.wait()
    total[...] = dot_nt(d_proj[...], w_in[...])
    scatter(info, total, (o0, o1, o2, o3))

    for j in range(4):
        shared[j, :, HD:] = d_state[:, j * HD : (j + 1) * HD]
    for k, out in enumerate((sh0, sh1, sh2, sh3)):
        out[...] = shared[(info[1] + k) % 4].astype(BF16)
    d_main[:, 0:KV0] = d_proj[:, 0:KV0]
    d_main[:, SH0:SH1] = jnp.zeros((rows, SH1 - SH0), BF16)
    d_main[:, SH1:] = d_proj[:, G0:S0]
    smalls[...] = jnp.zeros_like(smalls)
    smalls[0:8, :] = dot_tn(d_proj[:, T0:IN_COLS], x[...])[0:8]
    for j in range(4):
        smalls[8 + j : 9 + j, 0:INNER] = inner_taps[j]
        state_taps[j : j + 1, :] = jnp.zeros((1, state_taps.shape[1]), F32)
        state_taps[j : j + 1, 0 : 2 * STATE] = taps[j]
    smalls[12:13, 0:LANES] = jnp.sum(d_z, axis=0, keepdims=True)
    smalls[13:14, 0:LANES] = jnp.sum(-d_rate * step * decay, axis=0, keepdims=True)
    smalls[14:15, 0:INNER] = skip_cols


def feed_forward_kernel(
    layer, info, x0, x1, x2, x3, wg_own, wg_other, wu_own, wu_other, wd_own, wd_other,
    o0, o1, o2, o3, x_out, raw_out, w_gu, w_d, total, sems,
):
    units = w_d.shape[0]
    waits = [
        start_fetch(layer, info, wg_own, wg_other, w_gu.at[:, 0:units], sems.at[0]),
        start_fetch(layer, info, wu_own, wu_other, w_gu.at[:, units:], sems.at[1]),
    ]
    wait_d = start_fetch(layer, info, wd_own, wd_other, w_d, sems.at[2])
    assemble(info, (x0, x1, x2, x3), x_out)
    for item in waits:
        item.wait()
    raw_out[...] = dot_nn(x_out[...], w_gu[...])
    gate = raw_out[:, 0:units]
    hidden = (gate * sigmoid(gate) * raw_out[:, units:]).astype(BF16)
    wait_d.wait()
    total[...] = dot_nn(hidden, w_d[...])
    scatter(info, total, (o0, o1, o2, o3))


def feed_backward_kernel(
    layer, info, g0, g1, g2, g3, raw, wg_own, wg_other, wu_own, wu_other, wd_own, wd_other,
    o0, o1, o2, o3, g_out, d_raw, hidden, w_gu, w_d, total, sems,
):
    units = w_d.shape[0]
    wait_d = start_fetch(layer, info, wd_own, wd_other, w_d, sems.at[2])
    waits = [
        start_fetch(layer, info, wg_own, wg_other, w_gu.at[:, 0:units], sems.at[0]),
        start_fetch(layer, info, wu_own, wu_other, w_gu.at[:, units:], sems.at[1]),
    ]
    assemble(info, (g0, g1, g2, g3), g_out)
    gate, up = raw[:, 0:units], raw[:, units:]
    sig = sigmoid(gate)
    act = gate * sig
    hidden[...] = (act * up).astype(BF16)
    wait_d.wait()
    d_hidden = dot_nt(g_out[...], w_d[...])
    d_raw[:, 0:units] = (d_hidden * up * (sig * (1.0 + gate * (1.0 - sig)))).astype(BF16)
    d_raw[:, units:] = (d_hidden * act).astype(BF16)
    for item in waits:
        item.wait()
    total[...] = dot_nt(d_raw[...], w_gu[...])
    scatter(info, total, (o0, o1, o2, o3))


def sum_norm_kernel(
    layer, gain_row, narrow, info, h, p0, p1, p2, p3, small_own, small_other, total, normed, low
):
    small = pick(layer, info, small_own, small_other)
    value = h[...].astype(F32) + p0[...].astype(F32)
    for part in (p1, p2, p3):
        value = value + part[...].astype(F32)
    total[...] = value
    low[...] = value.astype(BF16)
    if narrow:
        value = low[...].astype(F32)
    r = lax.rsqrt(jnp.mean(value * value, axis=1, keepdims=True) + EPS)
    normed[...] = (value * r * small[gain_row : gain_row + 1]).astype(BF16)


def loss_grad_kernel(info, cotangent, grad, low):
    local = grad.shape[0]
    own = info[1] * local + iota((local, 1), 0)
    kept = (segment_of(own, sequence_ends(info)) < SEQS).astype(F32)
    value = cotangent[info[0]].astype(F32) * kept
    grad[...] = value
    low[...] = value.astype(BF16)


def norm_back_kernel(
    layer, gain_row, info, h, g, p0, p1, p2, p3, small_own, small_other, grad, low, d_gain
):
    small = pick(layer, info, small_own, small_other)
    d_normed = p0[...].astype(F32)
    for part in (p1, p2, p3):
        d_normed = d_normed + part[...].astype(F32)
    value = h[...].astype(F32)
    r = lax.rsqrt(jnp.mean(value * value, axis=1, keepdims=True) + EPS)
    n = value * r
    e = d_normed * small[gain_row : gain_row + 1]
    result = g[...].astype(F32) + r * (e - n * jnp.mean(e * n, axis=1, keepdims=True))
    grad[...] = result
    low[...] = result.astype(BF16)
    d_gain[...] = jnp.sum(d_normed * n, axis=0, keepdims=True)


def half_grads(half, joined, x, d, left, right, parts):
    span = x.shape[1] // 2
    side = left.shape[1] // 2
    xs = x[:, pl.ds(pl.multiple_of(half * span, span), span)]
    ls = left[:, pl.ds(pl.multiple_of(half * side, side), side)]
    grad = d[...]
    if joined:
        shared = sum_parts(parts).astype(BF16)
        grad = jnp.concatenate([grad[:, 0:SH0], shared, grad[:, SH1:]], axis=1)
    return dot_tn(xs, grad), dot_tn(ls, right[...])


def sum_parts(parts):
    total = parts[0][...].astype(F32)
    for part in parts[1:]:
        total = total + part[...].astype(F32)
    return total


def split_factors(groups, refs):
    refs, taken = list(refs), []
    for parts in groups:
        taken.append((refs[:4], refs[4 : 4 + parts]))
        refs = refs[4 + parts :]
    return taken, refs


def send_grad_kernel(groups, info, *rest):
    factors, (out,) = split_factors(groups, rest)
    at = 0
    for four, parts in factors:
        for grad in half_grads(1 - info[0], bool(parts), *four, parts):
            out[at : at + grad.shape[0]] = grad.astype(BF16)
            at += grad.shape[0]


def keep_grad_kernel(groups, info, arrived, *rest):
    factors, (out,) = split_factors(groups, rest)
    at = 0
    for four, parts in factors:
        for grad in half_grads(info[0], bool(parts), *four, parts):
            span = slice(at, at + grad.shape[0])
            out[span] = (grad + arrived[span].astype(F32)).astype(BF16)
            at += grad.shape[0]


def other_layer_kernel(info, second, feed, mixer, out, sems):
    size = feed.shape[0]

    @pl.when(info[0] == 0)
    def _():
        copy = pltpu.make_async_copy(second, out, sems.at[0])
        copy.start()
        copy.wait()

    @pl.when(info[0] != 0)
    def _():
        copies = [
            pltpu.make_async_copy(feed, out.at[0:size], sems.at[0]),
            pltpu.make_async_copy(mixer, out.at[size:], sems.at[1]),
        ]
        for copy in copies:
            copy.start()
        for copy in copies:
            copy.wait()


def spread_feed_kernel(info, own0, own1, other, gate, up, down, held, sems):
    span, side, units = gate.shape[0] // 2, down.shape[0] // 2, gate.shape[1]
    size = held.shape[0]
    wait = start_fetch(0, info, own0, own1.at[0:size], held, sems.at[0])

    def emit(half, source):
        rows = place(half, span)
        gate[rows, :] = source[0:span, 0:units].astype(F32)
        up[rows, :] = source[0:span, units:].astype(F32)
        down[place(half, side), :] = source[span:, :].astype(F32)

    emit(1 - info[0], other.at[0:size])
    wait.wait()
    emit(info[0], held)


def spread_mixer_kernel(info, own0, own1, other, *rest):
    query, gate, inner, attn_out, ssm_out, held, outs, sems = rest
    span, side = query.shape[0] // 2, outs.shape[0] // 2
    size = held.shape[0]
    wait = start_fetch(0, info, own0, own1.at[size:], held, sems.at[0])

    def emit(half, source):
        rows = place(half, span)
        query[rows, :] = source[0:span, 0:SH0].astype(F32)
        gate[rows, :] = source[0:span, SH1 : SH1 + INNER].astype(F32)
        inner[rows, :] = source[0:span, SH1 + INNER :].astype(F32)
        outs[place(half, side), :] = source[span:, :].astype(F32)

    emit(1 - info[0], other.at[size:])
    wait.wait()
    emit(info[0], held)
    attn_out[...] = outs[0:LANES]
    ssm_out[...] = outs[LANES:]


def spread_shared_kernel(info, p0, p1, p2, p3, key, value, state, shared):
    for k, piece in enumerate((p0, p1, p2, p3)):
        shared[(info[1] + k) % 4] = piece[...].astype(F32)
    for j in range(4):
        into = key if j < 2 else value
        into[:, (j % 2) * HD : (j % 2 + 1) * HD] = shared[j, :, 0:HD]
        state[:, j * HD : (j + 1) * HD] = shared[j, :, HD:]


def run(kernel, specs, args, shapes, scratch=(), flops=10**7, limit=16, after=(), far=()):
    shapes = [jax.ShapeDtypeStruct(*shape) for shape in shapes]
    taken, ordered = len(args), len(args) + len(after)
    given, private = ordered + len(shapes), ordered + len(shapes) + len(scratch)
    near = [i for i, spec in enumerate(specs) if spec is STREAM]
    buffers = [pltpu.VMEM(args[i].shape, args[i].dtype) for i in near]
    buffers += [pltpu.VMEM(shapes[i].shape, shapes[i].dtype) for i in far]
    if buffers:
        buffers.append(pltpu.SemaphoreType.DMA((len(near) + len(far),)))

    def moving_kernel(*refs):
        inputs, outputs = list(refs[:taken]), list(refs[ordered:given])
        copies = []
        for at, i in enumerate(near):
            held = refs[private + at]
            copies.append(pltpu.make_async_copy(inputs[i], held, refs[-1].at[at]))
            inputs[i] = held
        for copy in copies:
            copy.start()
        for copy in copies:
            copy.wait()
        copies = []
        for at, i in enumerate(far, len(near)):
            held = refs[private + at]
            copies.append(pltpu.make_async_copy(held, outputs[i], refs[-1].at[at]))
            outputs[i] = held
        kernel(*inputs, *outputs, *refs[given:private])
        for copy in copies:
            copy.start()
        for copy in copies:
            copy.wait()

    moved = sum(a.size * a.dtype.itemsize for a in list(args) + shapes)
    return list(pl.pallas_call(
        moving_kernel,
        out_shape=shapes,
        in_specs=[HBM if spec is STREAM else spec for spec in specs] + [ANY] * len(after),
        out_specs=[HBM if i in far else VMEM for i in range(len(shapes))],
        scratch_shapes=list(scratch) + buffers,
        compiler_params=pltpu.CompilerParams(vmem_limit_bytes=limit * MIB),
        cost_estimate=pl.CostEstimate(flops=flops, bytes_accessed=moved, transcendentals=0),
    )(*args, *after))


def gather_pieces(piece):
    size = lax.axis_size("tensor")
    return [piece] + [
        lax.ppermute(piece, "tensor", [(i, (i - k) % size) for i in range(size)])
        for k in range(1, size)
    ]


def scatter_pieces(pieces):
    size = lax.axis_size("tensor")
    return [pieces[0]] + [
        lax.ppermute(pieces[k], "tensor", [(i, (i + k) % size) for i in range(size)])
        for k in range(1, size)
    ]


def swap(value):
    return lax.ppermute(value, "section", [(0, 1), (1, 0)])


def dp_pairs(slot, k):
    size = lax.axis_size("dp")
    across = min(4, size)
    stride, count = (1, across) if slot == 2 else (across, size // across)
    pairs = []
    for i in range(size):
        at = i // stride % count
        pairs.append((i, i + ((at + k) % count - at) * stride))
    return pairs


def gather_dp(piece, slot):
    return [piece] + [lax.ppermute(piece, "dp", dp_pairs(slot, 4 - k)) for k in range(1, 4)]


def sum_over_dp(value):
    for slot in (2, 3):
        around = gather_dp(value, slot)
        value = around[0] + around[1] + around[2] + around[3]
    return value


def body(
    tokens,
    cotangent,
    seq_lengths,
    mix_gain,
    query_weight,
    key_weight,
    value_weight,
    attn_out_weight,
    ssm_gate_weight,
    ssm_in_weight,
    ssm_state_weight,
    ssm_step_weight,
    conv_inner,
    conv_state,
    step_bias,
    decay_log,
    skip_gain,
    ssm_out_weight,
    ffn_gain,
    ffn_gate_weight,
    ffn_up_weight,
    ffn_down_weight,
):
    section = lax.axis_index("section")
    tensor = lax.axis_index("tensor")
    local, width = tokens.shape[1], tokens.shape[2]
    rows = local * lax.axis_size("tensor")
    units = ffn_gate_weight.shape[2]
    mixed = attn_out_weight.shape[1] + ssm_out_weight.shape[1]

    dp = lax.axis_index("dp")
    across = min(4, lax.axis_size("dp"))
    place_here = jnp.stack([section, tensor, dp % across, dp // across]).astype(jnp.int32)
    info = jnp.concatenate([place_here, seq_lengths.reshape(-1)])

    def row(vector):
        return jnp.pad(vector, ((0, 0), (0, width - vector.shape[1])))

    small = jnp.concatenate(
        [
            jnp.pad(
                jnp.concatenate([conv_inner[0], conv_state[0]], axis=1),
                ((0, 0), (0, width - INNER - 2 * STATE)),
            ),
            row(step_bias),
            row(decay_log),
            row(jnp.repeat(skip_gain, SSM_DIM, axis=1)),
            mix_gain,
            ffn_gain,
            jnp.zeros((7, width), BF16),
        ],
        axis=0,
    )
    smalls_in = (small, swap(small))
    step_weight = jnp.pad(
        ssm_step_weight[0], ((0, 0), (0, LANES - ssm_step_weight.shape[2]))
    )
    packed = run(
        pack_kernel,
        [HBM] * 9,
        [
            query_weight[0],
            key_weight[0],
            value_weight[0],
            ssm_gate_weight[0],
            ssm_in_weight[0],
            ssm_state_weight[0],
            step_weight,
            attn_out_weight[0],
            ssm_out_weight[0],
        ],
        [((width, IN_COLS), BF16), ((mixed, width), BF16)],
        [pltpu.SemaphoreType.DMA((9,))],
        limit=60,
        far=(0, 1),
    )
    mixer_weights = [packed[0], swap(packed[0]), packed[1], swap(packed[1])]
    layer_in = lax.dynamic_index_in_dim(tokens, section, 0, keepdims=False)
    pieces = gather_pieces(layer_in)
    feed_weights = []
    for weight in (ffn_gate_weight[0], ffn_up_weight[0], ffn_down_weight[0]):
        feed_weights += [weight, swap(weight)]

    chunk32, chunk16 = ((local, width), F32), ((local, width), BF16)
    full16, full32 = ((rows, width), BF16), ((rows, width), F32)
    mixer_flops = 2 * rows * width * (IN_COLS + mixed)
    feed_flops = 2 * rows * width * 3 * units

    def mixer_scratch():
        return [
            pltpu.VMEM((width, IN_COLS), BF16),
            pltpu.VMEM((mixed, width), BF16),
            pltpu.VMEM((rows, width), F32),
        ]

    def feed_scratch():
        return [
            pltpu.VMEM((width, 2 * units), BF16),
            pltpu.VMEM((units, width), BF16),
            pltpu.VMEM((rows, width), F32),
            pltpu.SemaphoreType.DMA((3,)),
        ]

    loss_grad, loss_low = run(
        loss_grad_kernel, [SMEM, VMEM], [info, cotangent], [chunk32, chunk16]
    )
    loss_pieces = gather_pieces(loss_low)

    saved, layer_totals, layer_lows = [], [], []
    for layer in range(2):
        result = run(
            functools.partial(mixer_forward_kernel, layer),
            [SMEM] + [VMEM] * 6 + [HBM] * 4,
            [info, *pieces, *smalls_in, *mixer_weights],
            [chunk32] + [chunk16] * 3
            + [full16, ((rows, IN_COLS), F32), ((rows, INNER), F32), ((rows, mixed), BF16)],
            mixer_scratch() + [pltpu.SemaphoreType.DMA((2,))],
            mixer_flops,
            32,
            far=(4, 5, 6, 7),
        )
        x, proj, y, heads = result[4:]
        middle, normed, _ = run(
            functools.partial(sum_norm_kernel, layer, 8, False),
            [SMEM] + [VMEM] * 7,
            [info, layer_in, *scatter_pieces(result[:4]), *smalls_in],
            [chunk32, chunk16, chunk16],
        )
        result = run(
            functools.partial(feed_forward_kernel, layer),
            [SMEM] + [VMEM] * 4 + [HBM] * 6,
            [info, *gather_pieces(normed), *feed_weights],
            [chunk32] + [chunk16] * 3 + [full16, ((rows, 2 * units), F32)],
            feed_scratch(),
            feed_flops,
            32,
            far=(4, 5),
        )
        feed_x, feed_raw = result[4:]
        total, normed, low = run(
            functools.partial(sum_norm_kernel, 1, 7, True),
            [SMEM] + [VMEM] * 7,
            [info, middle, *scatter_pieces(result[:4]), *smalls_in],
            [chunk32, chunk16, chunk16],
        )
        if layer == 0:
            pieces = gather_pieces(normed)
        layer_totals.append(total)
        layer_lows.append(low)
        saved.append((layer_in, x, proj, y, heads, middle, feed_x, feed_raw))
        layer_in = low

    group = (width // 2 + units // 2, width)

    def send_grads(groups, after=()):
        operands = [item for group_items in groups for item in group_items]
        return run(
            functools.partial(send_grad_kernel, [len(items) - 4 for items in groups]),
            [SMEM] + grad_specs(groups),
            [info] + operands,
            [((len(groups) * group[0], width), BF16)],
            (),
            len(groups) * rows * width * (width + units),
            24,
            after=after,
        )[0]

    def grad_specs(groups):
        specs = []
        for items in groups:
            specs += [STREAM] * 4 + [VMEM] * (len(items) - 4)
        return specs

    def keep_grads(send, groups, after=()):
        operands = [item for group_items in groups for item in group_items]
        return run(
            functools.partial(keep_grad_kernel, [len(items) - 4 for items in groups]),
            [SMEM, VMEM] + grad_specs(groups),
            [info, swap(send)] + operands,
            [((len(groups) * group[0], width), BF16)],
            (),
            len(groups) * rows * width * (width + units),
            32,
            after=after,
        )

    grad, pieces = loss_grad, loss_pieces
    smalls, shared_smalls, grads_in, lows_in = {}, {}, {}, {}
    middle_after = []
    for layer in (1, 0):
        layer_in, x, proj, y, heads, middle, feed_x, feed_raw = saved[layer]
        result = run(
            functools.partial(feed_backward_kernel, layer),
            [SMEM] + [VMEM] * 4 + [STREAM] + [HBM] * 6,
            [info, *pieces, feed_raw, *feed_weights],
            [chunk32] + [chunk16] * 3 + [full16, full16, ((rows, units), BF16)],
            feed_scratch(),
            feed_flops,
            32,
            far=(4, 5, 6),
        )
        g_full, d_raw, hidden = result[4:]
        parts = scatter_pieces(result[:4])
        feed_factors = [feed_x, d_raw, hidden, g_full]
        if layer == 0:
            feed_send = send_grads([feed_factors])
            middle_after = [feed_send]
        d_middle, d_low, ffn_gain_grad = run(
            functools.partial(norm_back_kernel, layer, 8),
            [SMEM] + [VMEM] * 8,
            [info, middle, grad, *parts, *smalls_in],
            [chunk32, chunk16, ((1, width), F32)],
            after=middle_after,
        )
        if layer == 0:
            feed_kept = keep_grads(feed_send, [feed_factors])
            second_send = send_grads(second_groups, after=[d_low])
        result = run(
            functools.partial(mixer_backward_kernel, layer),
            [SMEM] + [VMEM] * 6 + [HBM] * 4 + [STREAM] * 3,
            [info, *gather_pieces(d_low), *smalls_in, *mixer_weights, x, proj, y],
            [chunk32] + [chunk16] * 3 + [((rows, LANES), BF16)] * 4
            + [full16, full16, ((16, width), F32), ((4, width), F32)],
            mixer_scratch()
            + [
                pltpu.VMEM((rows, IN_COLS), BF16),
                pltpu.VMEM((rows, INNER), F32),
                pltpu.VMEM((LANES, rows), F32),
                pltpu.VMEM((4, rows, LANES), F32),
                pltpu.SemaphoreType.DMA((2,)),
            ],
            2 * mixer_flops,
            40,
            after=feed_kept + [second_send] if layer == 0 else (),
            far=(8, 9),
        )
        parts = scatter_pieces(result[:4])
        g_full, d_main, smalls[layer], taps = result[8:]
        mixer_factors = [x, d_main, heads, g_full] + scatter_pieces(result[4:8])
        if layer == 1:
            second_groups = [feed_factors, mixer_factors]
        else:
            second_kept = keep_grads(second_send, second_groups)
            mixer_send = send_grads([mixer_factors], after=second_kept)
            mixer_kept = keep_grads(mixer_send, [mixer_factors])
            second, feed, mixer = lax.psum(
                (second_kept[0], feed_kept[0], mixer_kept[0]), "dp"
            )
        grad_in, grad, mix_gain_grad = run(
            functools.partial(norm_back_kernel, layer, 7),
            [SMEM] + [VMEM] * 8,
            [info, layer_in, d_middle, *parts, *smalls_in],
            [chunk32, chunk16, ((1, width), F32)],
        )
        grads_in[layer], lows_in[layer] = grad_in, grad
        shared_smalls[layer] = jnp.concatenate(
            [ffn_gain_grad, mix_gain_grad, taps, jnp.zeros((2, width), F32)], axis=0
        )
        if layer == 1:
            pieces = gather_pieces(grad)

    first = section == 0

    shared_pair = jnp.concatenate([shared_smalls[0], shared_smalls[1]], axis=0)
    around = gather_pieces(shared_pair)
    shared_pair = around[0] + around[1] + around[2] + around[3]
    by_layer = [
        jnp.concatenate([smalls[layer], shared_pair[8 * layer : 8 * layer + 8]], axis=0)
        for layer in range(2)
    ]
    small_sum = jnp.where(first, by_layer[0], by_layer[1]) + swap(
        jnp.where(first, by_layer[1], by_layer[0])
    )
    small_sum = sum_over_dp(small_sum)

    def to_layer(totals, lows):
        own_rows = jnp.where(first, totals[0], totals[1])
        other_rows = swap(jnp.where(first, lows[1], lows[0])).astype(F32)
        return jnp.stack(
            [jnp.where(first, own_rows, other_rows), jnp.where(first, other_rows, own_rows)]
        )[None]

    outputs = to_layer(layer_totals, layer_lows)
    inputs = to_layer(grads_in, lows_in)

    (sent,) = run(
        other_layer_kernel,
        [SMEM] + [HBM] * 3,
        [info, second, feed, mixer],
        [((2 * group[0], width), BF16)],
        [pltpu.SemaphoreType.DMA((2,))],
        10**6,
        56,
        after=[small_sum, outputs, inputs],
    )
    other = swap(sent)
    picked = slice(0, width // 2), slice(SH0, SH1)
    own_shared = jnp.where(first, mixer[picked], second[group[0] :][picked])
    other_shared = other[group[0] :][picked]
    shared = jnp.concatenate(
        [
            jnp.where(first, own_shared, other_shared),
            jnp.where(first, other_shared, own_shared),
        ],
        axis=0,
    )
    gate_grad, up_grad, down_grad = run(
        spread_feed_kernel,
        [SMEM, HBM, HBM, VMEM],
        [info, feed, second, other],
        [((width, units), F32), ((width, units), F32), ((units, width), F32)],
        [pltpu.VMEM(group, BF16), pltpu.SemaphoreType.DMA((1,))],
        10**6,
        56,
    )
    query_grad, gate_in_grad, inner_grad, ao_grad, so_grad = run(
        spread_mixer_kernel,
        [SMEM, HBM, HBM, VMEM],
        [info, mixer, second, other],
        [
            ((width, KV0), F32),
            ((width, INNER), F32),
            ((width, INNER), F32),
            ((LANES, width), F32),
            ((INNER, width), F32),
        ],
        [
            pltpu.VMEM(group, BF16),
            pltpu.VMEM((mixed, width), F32),
            pltpu.SemaphoreType.DMA((1,)),
        ],
        10**6,
        56,
    )
    key_grad, value_grad, state_grad = run(
        spread_shared_kernel,
        [SMEM] + [VMEM] * 4,
        [info, *gather_pieces(shared)],
        [
            ((width, KVH * HD), F32),
            ((width, KVH * HD), F32),
            ((width, 2 * STATE), F32),
        ],
        [pltpu.VMEM((4, width, LANES), F32)],
        10**6,
        24,
    )

    heads_here = step_bias.shape[1]
    return (
        outputs,
        inputs,
        small_sum[17:18],
        query_grad[None],
        key_grad[None],
        value_grad[None],
        ao_grad[None],
        gate_in_grad[None],
        inner_grad[None],
        state_grad[None],
        small_sum[0:heads_here].T[None],
        small_sum[8:12, 0:INNER][None],
        small_sum[18:22, 0 : 2 * STATE][None],
        small_sum[12:13, 0:heads_here],
        small_sum[13:14, 0:heads_here],
        jnp.sum(small_sum[14:15, 0:INNER].reshape(heads_here, SSM_DIM), axis=1)[None],
        so_grad[None],
        small_sum[16:17],
        gate_grad[None],
        up_grad[None],
        down_grad[None],
    )


def solution(mesh):
    placed = (
        P(None, ("dp", "tensor"), None),
        P(None, ("dp", "tensor"), None),
        P("dp", None, None),
        P("section", None),
        P("section", None, "tensor"),
        P("section", None, None),
        P("section", None, None),
        P("section", "tensor", None),
        P("section", None, "tensor"),
        P("section", None, "tensor"),
        P("section", None, None),
        P("section", None, "tensor"),
        P("section", None, "tensor"),
        P("section", None, None),
        P("section", "tensor"),
        P("section", "tensor"),
        P("section", "tensor"),
        P("section", "tensor", None),
        P("section", None),
        P("section", None, "tensor"),
        P("section", None, "tensor"),
        P("section", "tensor", None),
    )
    return jax.shard_map(
        body,
        mesh=mesh,
        in_specs=placed,
        out_specs=(
            P("section", None, ("dp", "tensor"), None),
            P("section", None, ("dp", "tensor"), None),
            P("section", None),
            P("section", None, "tensor"),
            P("section", None, None),
            P("section", None, None),
            P("section", "tensor", None),
            P("section", None, "tensor"),
            P("section", None, "tensor"),
            P("section", None, None),
            P("section", None, "tensor"),
            P("section", None, "tensor"),
            P("section", None, None),
            P("section", "tensor"),
            P("section", "tensor"),
            P("section", "tensor"),
            P("section", "tensor", None),
            P("section", None),
            P("section", None, "tensor"),
            P("section", None, "tensor"),
            P("section", "tensor", None),
        ),
        check_vma=False,
    )
```
